128 devices in a mesh: seq: 32 (over y, x, core), ch: 4 (over z).
Axes of the slice: x: 4, y: 4, z: 4, core: 2. Of those that a mesh axis runs over, the one named last changes fastest.
Arguments:
- qkv: bfloat16 [8192, 3, 4096], P('seq', None, 'ch'), may hold values from -6 to 6
- short_taps: float32 [3, 3, 4096], P(None, None, 'ch'), may hold values from -3 to 3
- lengths: int32 [8], replicated, may hold values from 1 to 2048, 8192 in all
- filter_taps: float32 [4, 1024, 2048], P('ch', 'seq'), may hold values from -2 to 2
- w_out: bfloat16 [4096, 4096], P(None, 'ch'), may hold values from -0.09375 to 0.09375
Outputs:
- mixed: bfloat16 [8192, 4096], P('seq', 'ch')
The draws below stay inside these ranges and needn't reach their ends.
Inputs may be any that keep to these rules, and one draw needn't show every extreme that they name: The lengths sum to 8192 and the longest is exactly 2048.
All inputs are finite; a program needn't handle non-finite values.
Results may differ from the reference program's by a relative error of at most 0.015.
Values may be sent and summed in bfloat16 or wider, within the bound.
No kernel may reach another device: no remote copies, remote signals or barrier semaphores. Data moves between devices by JAX's collectives and lax.ppermute only.
A program may use at most 128 MiB of HBM per device.

```python
import math
import jax
import jax.numpy as jnp
import numpy as np
from jax import lax

D = 4096
PROMPTS = 8
TAPS = 3
TOKENS = 8192
LMAX = 2048
CH_DEV = 1024


def draw_filter_taps(key, part):
    key = jax.random.fold_in(key, 7)
    keys = jax.random.split(key, 3)
    lowest = math.log(30.0)
    rates = jnp.exp(jax.random.uniform(keys[0], (D, 1), jnp.float32, lowest, math.log(32.0 * LMAX)))
    steps = jnp.arange(LMAX, dtype=jnp.float32)[None, :]
    scales = jnp.sqrt((1.0 - jnp.exp(-2.0 / rates)) / (1.0 - jnp.exp(-2.0 * LMAX / rates)))
    noise = jax.random.truncated_normal(keys[1], -4.0, 4.0, (D, LMAX), jnp.float32)
    far_noise = jax.random.truncated_normal(keys[2], -4.0, 4.0, (D, LMAX), jnp.float32)
    envelope = jnp.exp(-steps / rates)
    rising = (steps + 1.0) / LMAX
    far_shape = math.sqrt(2.5 / LMAX) * rising * rising
    near_share = math.sqrt(0.5)
    taps = near_share * scales * envelope * noise + far_shape * far_noise
    return taps.reshape(D // CH_DEV, CH_DEV, LMAX)


def steps_of(key, extent, pieces, smallest, largest):
    def one(axis_at, parts):
        draws = jax.random.uniform(jax.random.fold_in(jax.random.fold_in(key, 6), axis_at), (parts,), jnp.float32, smallest / len(pieces), largest / len(pieces))
        return jnp.repeat(jnp.exp(draws), extent[axis_at] // parts).reshape((-1,) + (1,) * (len(extent) - axis_at - 1))

    factor_of = one(*pieces[0])
    for cut in pieces[1:]:
        factor_of = factor_of * one(*cut)
    return factor_of


def profile(number_of, total, reach, slope):
    weights = [(1 << 20) // math.isqrt(rank ** slope) + 1 for rank in range(2, number_of + 1)]
    rest, holding = total - reach - (number_of - 1), [1] * (number_of - 1)
    while rest > 0:
        free = [i for i in range(number_of - 1) if holding[i] < reach]
        whole, left = sum([weights[i] for i in free]), rest
        for i in free:
            extra = min(reach - holding[i], max(1, left * weights[i] // whole), rest)
            holding[i] = holding[i] + extra
            rest = rest - extra
    return np.array([reach] + holding)


def uneven(rng, amount, total, bound, lean):
    if amount == 2:
        one = jax.random.randint(rng, (), max(1, total - bound), min(bound, total - 1) + 1)
        return jnp.stack([one, total - one])
    sizes = jnp.asarray(profile(amount, total, bound, lean), jnp.int32)
    couples = (amount - 1) // 2
    donor, taker = sizes[1:1 + 2 * couples:2], sizes[2:2 + 2 * couples:2]
    margin = jnp.minimum(donor - 1, bound - taker)
    passed = jax.random.randint(jax.random.fold_in(rng, 1), (couples,), 0, 1 << 20) % (margin + 1)
    sizes = sizes.at[1:1 + 2 * couples:2].set(donor - passed).at[2:2 + 2 * couples:2].set(taker + passed)
    return sizes[jax.random.permutation(jax.random.fold_in(rng, 2), amount)]


def normal_values(rng, dims, spread, limit, shards=(), kind=jnp.bfloat16):
    values = spread * jax.random.normal(rng, dims, jnp.float32)
    if shards:
        values = values * steps_of(rng, dims, shards, -0.22, 0.18)
    return jnp.clip(values, -limit, limit).astype(kind)


def setup_inputs(seed: int = 0) -> dict:
    seeds = jax.random.split(jax.random.key(seed), 6)
    return {
        "qkv": normal_values(seeds[0], (TOKENS, 3, D), 1.0, 6.0, ((0, 32), (2, 4))),
        "short_taps": normal_values(seeds[1], (TAPS, 3, D), 0.6, 3.0, ((2, 4),), jnp.float32),
        "lengths": uneven(seeds[2], PROMPTS, TOKENS, LMAX, 2).astype(jnp.int32),
        "filter_taps": draw_filter_taps(jax.random.fold_in(seeds[5], 71), 0),
        "w_out": normal_values(seeds[4], (D, D), D ** -0.5, 0.09375, ((1, 4),)),
    }


def prompt_starts(lengths, total):
    offsets = (jnp.cumsum(lengths) - lengths).astype(jnp.int32)
    positions = jnp.arange(total, dtype=jnp.int32)
    starts = jnp.max(jnp.where(offsets[None, :] <= positions[:, None], offsets[None, :], 0), axis=1)
    return offsets, positions, starts


def long_conv(signal, taps, offsets, lengths):
    channels, total = signal.shape
    span = taps.shape[1]
    size_n = 2 * span
    spectrum = jnp.fft.rfft(taps, n=size_n, axis=1)
    padded = jnp.concatenate([signal, jnp.zeros((channels, span), jnp.float32)], 1)
    result = jnp.zeros((channels, total + span), jnp.float32)
    steps = jnp.arange(span, dtype=jnp.int32)
    for prompt in range(lengths.shape[0]):
        live = (steps < lengths[prompt]).astype(jnp.float32)
        piece = lax.dynamic_slice_in_dim(padded, offsets[prompt], span, 1) * live[None, :]
        output = jnp.fft.irfft(jnp.fft.rfft(piece, n=size_n, axis=1) * spectrum, n=size_n, axis=1)[:, :span]
        output = output * live[None, :]
        current = lax.dynamic_slice_in_dim(result, offsets[prompt], span, 1)
        result = lax.dynamic_update_slice_in_dim(result, current + output, offsets[prompt], 1)
    return result[:, :total]


def reference(qkv, short_taps, lengths, filter_taps, w_out):
    total = qkv.shape[0]
    offsets, positions, starts = prompt_starts(lengths, total)
    padded = jnp.concatenate([jnp.zeros((TAPS - 1,) + qkv.shape[1:], qkv.dtype), qkv], 0)
    filtered = jnp.zeros(qkv.shape, jnp.float32)
    for tap_index in range(TAPS):
        window = padded[TAPS - 1 - tap_index:TAPS - 1 - tap_index + total].astype(jnp.float32)
        keep = ((positions - tap_index) >= starts).astype(jnp.float32)
        filtered = filtered + short_taps[tap_index][None] * window * keep[:, None, None]
    query = filtered[:, 0, :].astype(jnp.bfloat16)
    product = (filtered[:, 1, :] * filtered[:, 2, :]).astype(jnp.bfloat16)
    conv = long_conv(product.T.astype(jnp.float32), filter_taps.reshape(D, LMAX), offsets, lengths)
    conv_b = conv.astype(jnp.bfloat16)
    gated = (query.astype(jnp.float32) * conv_b.T.astype(jnp.float32)).astype(jnp.bfloat16)
    return jnp.dot(gated, w_out, preferred_element_type=jnp.float32).astype(jnp.bfloat16)
```

```python
import functools

import jax
import jax.numpy as jnp
from jax import lax
from jax.experimental import pallas as pl
from jax.experimental.pallas import tpu as pltpu
from jax.sharding import PartitionSpec as P

TAPS = 3
BLK = 128
MIB = 1 << 20


def params(mib):
    return pltpu.CompilerParams(vmem_limit_bytes=mib * MIB)


def starts_of(lengths_ref, positions):
    starts = jnp.zeros(positions.shape, jnp.int32)
    offset = jnp.int32(0)
    for prompt in range(lengths_ref.shape[0]):
        starts = jnp.where(positions >= offset, offset, starts)
        offset = offset + lengths_ref[prompt]
    return starts


def short_filter(scr, taps_ref, which, keeps, tok_rows):
    total = None
    for tap in range(TAPS):
        term = taps_ref[tap, which : which + 1, :] * scr[8 - tap : 8 - tap + tok_rows, :] * keeps[tap]
        total = term if total is None else total + term
    return total


def fill(scr, tok_rows, edge, values):
    scr[6:8, :] = edge.astype(jnp.float32)
    scr[8 : 8 + tok_rows, :] = values.astype(jnp.float32)


def keep_masks(lengths_ref, tok_rows, width):
    place = lax.axis_index("seq") * tok_rows
    positions = place + lax.broadcasted_iota(jnp.int32, (tok_rows, width), 0)
    starts = starts_of(lengths_ref, positions)
    return [(positions - tap >= starts).astype(jnp.float32) for tap in range(TAPS)]


def product_kernel(lengths_ref, kv_ref, edge_ref, taps_ref, out_ref, scr_k, scr_v):
    tok_rows, width = kv_ref.shape[1:]
    keeps = keep_masks(lengths_ref, tok_rows, width)
    fill(scr_k, tok_rows, edge_ref[:, 1, :], kv_ref[1])
    fill(scr_v, tok_rows, edge_ref[:, 2, :], kv_ref[2])
    product = short_filter(scr_k, taps_ref, 1, keeps, tok_rows) * short_filter(
        scr_v, taps_ref, 2, keeps, tok_rows
    )
    out_ref[...] = product.T.astype(jnp.bfloat16)


def query_kernel(lengths_ref, q_ref, edge_ref, taps_ref, out_ref, scr_q):
    tok_rows, width = q_ref.shape[1:]
    keeps = keep_masks(lengths_ref, tok_rows, width)
    fill(scr_q, tok_rows, edge_ref[:, 0, :], q_ref[0])
    out_ref[...] = short_filter(scr_q, taps_ref, 0, keeps, tok_rows).astype(jnp.bfloat16)


def short_call(kernel, lengths, qkv, edge, taps, transposed, scratches, width=256):
    parts, tok_rows, channels = qkv.shape
    if transposed:
        shape, spec = (channels, tok_rows), pl.BlockSpec((width, tok_rows), lambda i: (i, 0))
    else:
        shape, spec = (tok_rows, channels), pl.BlockSpec((tok_rows, width), lambda i: (0, i))
    return pl.pallas_call(
        kernel,
        grid=(channels // width,),
        out_shape=jax.ShapeDtypeStruct(shape, jnp.bfloat16),
        in_specs=[
            pl.BlockSpec(memory_space=pltpu.SMEM),
            pl.BlockSpec((parts, tok_rows, width), lambda i: (0, 0, i)),
            pl.BlockSpec((TAPS - 1, 3, width), lambda i: (0, 0, i)),
            pl.BlockSpec((TAPS, 3, width), lambda i: (0, 0, i)),
        ],
        out_specs=spec,
        scratch_shapes=[pltpu.VMEM((tok_rows + 8, width), jnp.float32)] * scratches,
        compiler_params=params(32),
        cost_estimate=pl.CostEstimate(flops=20 * tok_rows * channels, bytes_accessed=4 * MIB, transcendentals=0),
    )(lengths, qkv, edge, taps)


def toeplitz_kernel(taps_ref, out_ref):
    count, span = taps_ref.shape
    for c in range(count):
        row = jnp.concatenate([taps_ref[c : c + 1, :], jnp.zeros((1, BLK), jnp.float32)], 1)
        wide = jnp.broadcast_to(row, (BLK, span + BLK))
        sheared = pltpu.roll(wide, 0, 1, stride=1, stride_axis=0)
        for t in range(span // BLK + 1):
            out_ref[c, t * BLK : (t + 1) * BLK, :] = sheared[:, t * BLK : (t + 1) * BLK].astype(jnp.bfloat16)


def toeplitz(taps, group=8):
    channels, span = taps.shape
    depth = span + BLK
    return pl.pallas_call(
        toeplitz_kernel,
        grid=(channels // group,),
        out_shape=jax.ShapeDtypeStruct((channels, depth, BLK), jnp.bfloat16),
        in_specs=[pl.BlockSpec((group, span), lambda i: (i, 0))],
        out_specs=pl.BlockSpec((group, depth, BLK), lambda i: (i, 0, 0)),
        compiler_params=params(32),
        cost_estimate=pl.CostEstimate(
            flops=8 * channels * depth * BLK, bytes_accessed=2 * channels * depth * BLK, transcendentals=0
        ),
    )(taps)


def over_rows(lengths_ref, body):
    def prompt_step(prompt, carry):
        offset, row = carry
        end = offset + lengths_ref[prompt]
        first, last = offset // BLK, (end - 1) // BLK

        def block_step(block, _):
            body(row + block - first, block, offset, end)
            return 0

        lax.fori_loop(first, last + 1, block_step, 0)
        return end, row + last - first + 1

    lax.fori_loop(0, lengths_ref.shape[0], prompt_step, (jnp.int32(0), jnp.int32(0)))


def lanes_of(block, start, end, rows):
    positions = block * BLK + lax.broadcasted_iota(jnp.int32, (rows, BLK), 1)
    return (positions >= start) & (positions < end)


def conv_kernel(
    lengths_ref, signal_ref, toep_ref, out_ref, blocks, spread, masks, lhs, result, *, rows, rows_b, lags
):
    step = pl.program_id(0)
    devices, channels, tok_rows = signal_ref.shape
    group = toep_ref.shape[0]
    per = tok_rows // BLK
    pad = lags - 1
    pitch = pad + rows_b

    @pl.when(step == 0)
    def _():
        for device in range(devices):
            for part in range(per):
                blocks[device * per + part] = signal_ref[
                    device, :, part * BLK : (part + 1) * BLK
                ].astype(jnp.float32)
        spread[...] = jnp.zeros_like(spread)

        def place(row, block, start, end):
            slab = jnp.where(lanes_of(block, start, end, channels), blocks[block], 0.0)
            spread[pl.ds(pad + row, channels, stride=pitch), :] = slab

        over_rows(lengths_ref, place)
        row_ids = lax.broadcasted_iota(jnp.int32, (rows_b, BLK), 0)
        firsts = jnp.zeros((rows_b, BLK), jnp.int32)
        offset, row = jnp.int32(0), jnp.int32(0)
        for prompt in range(lengths_ref.shape[0]):
            firsts = jnp.where(row_ids >= row, row, firsts)
            end = offset + lengths_ref[prompt]
            row = row + (end - 1) // BLK - offset // BLK + 1
            offset = end
        for lag in range(lags):
            masks[lag] = (row_ids - lag >= firsts).astype(jnp.float32)

    views = spread.reshape(channels, pitch, BLK)
    for g in range(group):
        channel = step * group + g
        for lag in range(lags):
            shifted = views[channel, pad - lag : pad - lag + rows_b, :]
            lhs[g, :, lag * BLK : (lag + 1) * BLK] = (shifted * masks[lag]).astype(jnp.bfloat16)
        total = jnp.dot(lhs[g], toep_ref[g], preferred_element_type=jnp.float32)
        result[pl.ds(channel * rows, rows), :] = total[:rows]

    @pl.when(step == pl.num_programs(0) - 1)
    def _():
        def collect(row, block, start, end):
            slab = result[pl.ds(row, channels, stride=rows), :]
            blocks[block] = jnp.where(lanes_of(block, start, end, channels), slab, blocks[block])

        over_rows(lengths_ref, collect)
        for device in range(devices):
            for part in range(per):
                out_ref[device, :, part * BLK : (part + 1) * BLK] = blocks[device * per + part].astype(jnp.bfloat16)


def long_conv(lengths, signal, toep, group=2):
    devices, channels, tok_rows = signal.shape
    total = devices * tok_rows
    depth = toep.shape[1]
    lags = depth // BLK
    rows = -(-(total // BLK + lengths.shape[0] - 1) // 8) * 8
    rows_b = -(-rows // 16) * 16
    pitch = lags - 1 + rows_b
    return pl.pallas_call(
        functools.partial(conv_kernel, rows=rows, rows_b=rows_b, lags=lags),
        grid=(channels // group,),
        out_shape=jax.ShapeDtypeStruct(signal.shape, jnp.bfloat16),
        in_specs=[
            pl.BlockSpec(memory_space=pltpu.SMEM),
            pl.BlockSpec(signal.shape, lambda i: (0, 0, 0)),
            pl.BlockSpec((group, depth, BLK), lambda i: (i, 0, 0)),
        ],
        out_specs=pl.BlockSpec(signal.shape, lambda i: (0, 0, 0)),
        scratch_shapes=[
            pltpu.VMEM((total // BLK, channels, BLK), jnp.float32),
            pltpu.VMEM((channels * pitch, BLK), jnp.float32),
            pltpu.VMEM((lags, rows_b, BLK), jnp.float32),
            pltpu.VMEM((group, rows_b, depth), jnp.bfloat16),
            pltpu.VMEM((channels * rows, BLK), jnp.float32),
        ],
        compiler_params=params(40),
        cost_estimate=pl.CostEstimate(
            flops=2 * channels * rows * depth * BLK, bytes_accessed=2 * channels * depth * BLK, transcendentals=0
        ),
    )(lengths, signal, toep)


def gate_kernel(query_ref, conv_ref, out_ref):
    conv = conv_ref[...].astype(jnp.float32).T
    out_ref[...] = (query_ref[...].astype(jnp.float32) * conv).astype(jnp.bfloat16)


def gate(query, conv_t, width=256):
    tok_rows, channels = query.shape
    return pl.pallas_call(
        gate_kernel,
        grid=(channels // width,),
        out_shape=jax.ShapeDtypeStruct(query.shape, jnp.bfloat16),
        in_specs=[
            pl.BlockSpec((tok_rows, width), lambda i: (0, i)),
            pl.BlockSpec((width, tok_rows), lambda i: (i, 0)),
        ],
        out_specs=pl.BlockSpec((tok_rows, width), lambda i: (0, i)),
        compiler_params=params(32),
        cost_estimate=pl.CostEstimate(flops=tok_rows * channels, bytes_accessed=2 * MIB, transcendentals=0),
    )(query, conv_t)


def shift(array, axis, by):
    length = lax.axis_size(axis)
    return lax.ppermute(array, axis, [(i, (i + by) % length) for i in range(length)])


def project(gated, w_out):
    size = lax.axis_size("ch")
    depth = gated.shape[1]
    place = lax.axis_index("ch")

    def part(block, owner):
        rows = lax.dynamic_slice_in_dim(w_out, owner % size * depth, depth, 0)
        return jnp.dot(block, rows, preferred_element_type=jnp.float32)

    half = gated.shape[0] // 2
    right, left = shift(gated, "ch", 1), shift(gated, "ch", -1)
    far = jnp.concatenate([shift(right[:half], "ch", 1), shift(left[half:], "ch", -1)], 0)
    total = part(gated, place) + part(right, place + size - 1) + part(left, place + 1)
    return (total + part(far, place + 2)).astype(jnp.bfloat16)


def per_device(qkv, short_taps, lengths, filter_taps, w_out):
    tok_rows, _, width = qkv.shape
    lead = TAPS - 1
    seq = lax.axis_size("seq")
    edge = lax.ppermute(qkv[tok_rows - lead :], "seq", [(i, i + 1) for i in range(seq - 1)])
    by_kind = qkv.transpose(1, 0, 2)
    product_t = short_call(product_kernel, lengths, by_kind, edge, short_taps, True, 2)
    query = short_call(query_kernel, lengths, by_kind, edge, short_taps, False, 1)
    toep = toeplitz(filter_taps[0])
    signal = lax.all_to_all(product_t.reshape(seq, width // seq, tok_rows), "seq", 0, 0, tiled=True)
    conv = long_conv(lengths, signal, toep)
    conv_t = lax.all_to_all(conv, "seq", 0, 0, tiled=True).reshape(width, tok_rows)
    return project(gate(query, conv_t), w_out)


def solution(mesh):
    placed = (P("seq", None, "ch"), P(None, None, "ch"), P(), P("ch", "seq", None), P(None, "ch"))
    return jax.shard_map(
        per_device, mesh=mesh, in_specs=placed, out_specs=P("seq", "ch"), check_vma=False
    )
```

```python
import functools

import jax
import jax.numpy as jnp
from jax import lax
from jax.experimental import pallas as pl
from jax.experimental.pallas import tpu as pltpu
from jax.sharding import PartitionSpec as P

TAPS = 3
BLK = 256
TILE = 128
PAD = 8
GRANT = 24
MIB = 1 << 20


def params(mib):
    return pltpu.CompilerParams(vmem_limit_bytes=mib * MIB)


def short_filter(scr, taps_ref, which, keeps_ref, lanes):
    tok_rows = scr.shape[0] - 8
    total = taps_ref[0, which : which + 1, lanes] * scr[8 : 8 + tok_rows, lanes]
    for tap in range(1, TAPS):
        window = scr[8 - tap : 8 - tap + tok_rows, lanes] * keeps_ref[tap - 1]
        total = total + taps_ref[tap, which : which + 1, lanes] * window
    return total


def fill(scr, edge, values):
    scr[6:8, :] = edge.astype(jnp.float32)
    scr[8:, :] = values.astype(jnp.float32)


def fill_keeps(lengths_ref, keeps_ref):
    @pl.when(pl.program_id(0) == 0)
    def _():
        _, tok_rows, width = keeps_ref.shape
        place = lax.axis_index("seq") * tok_rows
        positions = place + lax.broadcasted_iota(jnp.int32, (tok_rows, width), 0)
        starts = jnp.zeros((tok_rows, width), jnp.int32)
        offset = jnp.int32(0)
        for prompt in range(lengths_ref.shape[0]):
            starts = jnp.where(positions >= offset, offset, starts)
            offset = offset + lengths_ref[prompt]
        for tap in range(1, TAPS):
            keeps_ref[tap - 1] = (positions - tap >= starts).astype(jnp.float32)


def lane_parts(width):
    return [slice(i, i + TILE) for i in range(0, width, TILE)]


def product_kernel(lengths_ref, k_ref, v_ref, edge_ref, taps_ref, out_ref, keeps_ref, scr_k, scr_v):
    fill_keeps(lengths_ref, keeps_ref)
    fill(scr_k, edge_ref[:, 1, :], k_ref[...])
    fill(scr_v, edge_ref[:, 2, :], v_ref[...])
    for lanes in lane_parts(k_ref.shape[1]):
        product = short_filter(scr_k, taps_ref, 1, keeps_ref, lanes) * short_filter(
            scr_v, taps_ref, 2, keeps_ref, lanes
        )
        out_ref[lanes, :] = product.T.astype(jnp.bfloat16)


def query_kernel(lengths_ref, q_ref, edge_ref, taps_ref, out_ref, keeps_ref, scr_q):
    fill_keeps(lengths_ref, keeps_ref)
    fill(scr_q, edge_ref[:, 0, :], q_ref[...])
    for lanes in lane_parts(q_ref.shape[1]):
        out_ref[:, lanes] = short_filter(scr_q, taps_ref, 0, keeps_ref, lanes).astype(jnp.bfloat16)


def short_call(kernel, lengths, by_kind, edge, taps, kinds, transposed, width=256):
    _, tok_rows, channels = by_kind.shape
    if transposed:
        shape, spec = (channels, tok_rows), pl.BlockSpec((width, tok_rows), lambda i: (i, 0))
    else:
        shape, spec = (tok_rows, channels), pl.BlockSpec((tok_rows, width), lambda i: (0, i))
    return pl.pallas_call(
        kernel,
        grid=(channels // width,),
        out_shape=jax.ShapeDtypeStruct(shape, jnp.bfloat16),
        in_specs=[pl.BlockSpec(memory_space=pltpu.SMEM)]
        + [pl.BlockSpec((None, tok_rows, width), lambda i, kind=kind: (kind, 0, i)) for kind in kinds]
        + [
            pl.BlockSpec((TAPS - 1, 3, width), lambda i: (0, 0, i)),
            pl.BlockSpec((TAPS, 3, width), lambda i: (0, 0, i)),
        ],
        out_specs=spec,
        scratch_shapes=[pltpu.VMEM((TAPS - 1, tok_rows, TILE), jnp.float32)]
        + [pltpu.VMEM((tok_rows + 8, width), jnp.float32)] * len(kinds),
        compiler_params=params(GRANT),
        cost_estimate=pl.CostEstimate(flops=20 * tok_rows * channels, bytes_accessed=2 * MIB, transcendentals=0),
    )(lengths, *([by_kind] * len(kinds)), edge, taps)


def over_rows(lengths_ref, body):
    def prompt_step(prompt, carry):
        offset, row = carry
        end = offset + lengths_ref[prompt]
        first, last = offset // BLK, (end - 1) // BLK

        def block_step(block, _):
            body(row + block - first, block, offset, end)
            return 0

        lax.fori_loop(first, last + 1, block_step, 0)
        return end, row + last - first + 1

    lax.fori_loop(0, lengths_ref.shape[0], prompt_step, (jnp.int32(0), jnp.int32(0)))


def rows_before(lengths_ref, rows):
    row_ids = lax.broadcasted_iota(jnp.int32, (rows, TILE), 0)
    firsts = jnp.zeros((rows, TILE), jnp.int32)
    offset, row = jnp.int32(0), jnp.int32(0)
    for prompt in range(lengths_ref.shape[0]):
        firsts = jnp.where(row_ids >= row, row, firsts)
        end = offset + lengths_ref[prompt]
        row = row + (end - 1) // BLK - offset // BLK + 1
        offset = end
    return row_ids - firsts


def lanes_of(block, start, end, rows):
    positions = block * BLK + lax.broadcasted_iota(jnp.int32, (rows, BLK), 1)
    return (positions >= start) & (positions < end)


def conv_kernel(lengths_ref, signal_ref, taps_ref, out_ref, spread, result, before, toep, *, rows, rows_b):
    step = pl.program_id(0)
    devices, channels, _ = signal_ref.shape
    group, span = taps_ref.shape
    lags = span // BLK + 1
    tiles = span // TILE + 1
    pitch = PAD + rows_b

    @pl.when(step == 0)
    def _():
        def place(row, block, start, end):
            slab = jnp.where(lanes_of(block, start, end, channels), signal_ref[block].astype(jnp.float32), 0.0)
            for h in range(2):
                spread[h, pl.ds(PAD + row, channels, stride=pitch), :] = slab[:, h * TILE : (h + 1) * TILE]

        over_rows(lengths_ref, place)
        before[...] = rows_before(lengths_ref, rows_b)

    views = spread.reshape(2, channels, pitch, TILE)
    zero = jnp.zeros((TILE, TILE), jnp.bfloat16)
    behind = before[...]

    def tile(g, t):
        return toep[g, t * TILE : (t + 1) * TILE, :] if 0 <= t < tiles else zero

    for g in range(group):
        channel = step * group + g
        row = jnp.concatenate([taps_ref[g : g + 1, :], jnp.zeros((1, TILE), jnp.float32)], 1)
        sheared = pltpu.roll(jnp.broadcast_to(row, (TILE, span + TILE)), 0, 1, stride=1, stride_axis=0)
        for t in range(tiles):
            toep[g, t * TILE : (t + 1) * TILE, :] = sheared[:, t * TILE : (t + 1) * TILE].astype(jnp.bfloat16)
        total = None
        for lag in range(lags):
            kept = behind >= lag
            left = jnp.concatenate(
                [
                    jnp.where(kept, views[h, channel, PAD - lag : PAD - lag + rows_b, :], 0.0).astype(jnp.bfloat16)
                    for h in range(2)
                ],
                1,
            )
            t = 2 * lag
            right = jnp.concatenate(
                [
                    jnp.concatenate([tile(g, t), tile(g, t + 1)], 1),
                    jnp.concatenate([tile(g, t - 1), tile(g, t)], 1),
                ],
                0,
            )
            term = jnp.dot(left, right, preferred_element_type=jnp.float32)
            total = term if total is None else total + term
        for h in range(2):
            result[h, pl.ds(channel * rows, rows), :] = total[:rows, h * TILE : (h + 1) * TILE]

    @pl.when(step == pl.num_programs(0) - 1)
    def _():
        def collect(row, block, start, end):
            slab = jnp.concatenate([result[h, pl.ds(row, channels, stride=rows), :] for h in range(2)], 1)
            old = out_ref[block].astype(jnp.float32)
            out_ref[block] = jnp.where(lanes_of(block, start, end, channels), slab, old).astype(jnp.bfloat16)

        over_rows(lengths_ref, collect)


def long_conv(lengths, signal, taps, group=16):
    devices, channels, _ = signal.shape
    span = taps.shape[1]
    rows = -(-(devices + lengths.shape[0] - 1) // 8) * 8
    rows_b = -(-rows // 16) * 16
    return pl.pallas_call(
        functools.partial(conv_kernel, rows=rows, rows_b=rows_b),
        grid=(channels // group,),
        out_shape=jax.ShapeDtypeStruct(signal.shape, jnp.bfloat16),
        in_specs=[
            pl.BlockSpec(memory_space=pltpu.SMEM),
            pl.BlockSpec(signal.shape, lambda i: (0, 0, 0)),
            pl.BlockSpec((group, span), lambda i: (i, 0)),
        ],
        out_specs=pl.BlockSpec(signal.shape, lambda i: (0, 0, 0)),
        scratch_shapes=[
            pltpu.VMEM((2, channels * (PAD + rows_b), TILE), jnp.float32),
            pltpu.VMEM((2, channels * rows, TILE), jnp.float32),
            pltpu.VMEM((rows_b, TILE), jnp.int32),
            pltpu.VMEM((group, span + TILE, TILE), jnp.bfloat16),
        ],
        compiler_params=params(GRANT),
        cost_estimate=pl.CostEstimate(
            flops=2 * channels * rows * (span + BLK) * BLK, bytes_accessed=2 * MIB, transcendentals=0
        ),
    )(lengths, signal, taps)


def gate_kernel(query_ref, conv_ref, *out_refs):
    conv = conv_ref[...].astype(jnp.float32).T
    gated = (query_ref[...].astype(jnp.float32) * conv).astype(jnp.bfloat16)
    rows = gated.shape[0] // len(out_refs)
    for i, out_ref in enumerate(out_refs):
        out_ref[...] = gated[i * rows : (i + 1) * rows]


def gate(query, conv_t, pieces=2, width=256):
    tok_rows, channels = query.shape
    rows = tok_rows // pieces
    return pl.pallas_call(
        gate_kernel,
        grid=(channels // width,),
        out_shape=[jax.ShapeDtypeStruct((rows, channels), jnp.bfloat16)] * pieces,
        in_specs=[
            pl.BlockSpec((tok_rows, width), lambda i: (0, i)),
            pl.BlockSpec((width, tok_rows), lambda i: (i, 0)),
        ],
        out_specs=[pl.BlockSpec((rows, width), lambda i: (0, i))] * pieces,
        compiler_params=params(GRANT),
        cost_estimate=pl.CostEstimate(flops=tok_rows * channels, bytes_accessed=2 * MIB, transcendentals=0),
    )(query, conv_t)


def shift(array, axis, by):
    length = lax.axis_size(axis)
    return lax.ppermute(array, axis, [(i, (i + by) % length) for i in range(length)])


def project_kernel(*refs, count, pieces, has_total):
    blocks, weights = refs[: count * pieces], refs[count * pieces : count * (pieces + 1)]
    out_ref = refs[-1]
    total = refs[count * (pieces + 1)][...] if has_total else None
    for i in range(count):
        block = jnp.concatenate([ref[...] for ref in blocks[i * pieces : (i + 1) * pieces]], 0)
        term = jnp.dot(block, weights[i][...], preferred_element_type=jnp.float32)
        total = term if total is None else total + term
    out_ref[...] = total.astype(out_ref.dtype)


def project_part(blocks, weights, total, kind):
    count, pieces = len(blocks), len(blocks[0])
    rows, depth = blocks[0][0].shape
    columns = weights[0].shape[1]
    tok_rows = rows * pieces
    operands = [piece for block in blocks for piece in block] + weights + ([] if total is None else [total])
    return pl.pallas_call(
        functools.partial(project_kernel, count=count, pieces=pieces, has_total=total is not None),
        out_shape=jax.ShapeDtypeStruct((tok_rows, columns), kind),
        compiler_params=params(GRANT),
        cost_estimate=pl.CostEstimate(
            flops=2 * count * tok_rows * depth * columns,
            bytes_accessed=2 * count * depth * columns,
            transcendentals=0,
        ),
    )(*operands)


def project(pieces, w_out):
    size = lax.axis_size("ch")
    place = lax.axis_index("ch")
    depth = pieces[0].shape[1]
    own, after, far_rows, before = (
        lax.dynamic_slice_in_dim(w_out, (place + i) % size * depth, depth, 0) for i in range(size)
    )
    up, down = pieces
    right_up, left_down = shift(up, "ch", 1), shift(down, "ch", -1)
    right_down, left_up = shift(down, "ch", 1), shift(up, "ch", -1)
    far_up, far_down = shift(right_up, "ch", 1), shift(left_down, "ch", -1)
    total = project_part([(up, down)], [own], None, jnp.float32)
    near = [(right_up, right_down), (left_up, left_down)]
    total = project_part(near, [before, after], total, jnp.float32)
    return project_part([(far_up, far_down)], [far_rows], total, jnp.bfloat16)


def per_device(qkv, short_taps, lengths, filter_taps, w_out):
    tok_rows, _, width = qkv.shape
    lead = TAPS - 1
    seq = lax.axis_size("seq")
    edge = lax.ppermute(qkv[tok_rows - lead :], "seq", [(i, i + 1) for i in range(seq - 1)])
    by_kind = qkv.transpose(1, 0, 2)
    product_t = short_call(product_kernel, lengths, by_kind, edge, short_taps, (1, 2), True)
    query = short_call(query_kernel, lengths, by_kind, edge, short_taps, (0,), False)
    signal = lax.all_to_all(product_t.reshape(seq, width // seq, tok_rows), "seq", 0, 0, tiled=True)
    conv = long_conv(lengths, signal, filter_taps[0])
    conv_t = lax.all_to_all(conv, "seq", 0, 0, tiled=True).reshape(width, tok_rows)
    return project(gate(query, conv_t), w_out)


def solution(mesh):
    placed = (P("seq", None, "ch"), P(None, None, "ch"), P(), P("ch", "seq", None), P(None, "ch"))
    return jax.shard_map(
        per_device, mesh=mesh, in_specs=placed, out_specs=P("seq", "ch"), check_vma=False
    )
```

```python
import functools

import jax
import jax.numpy as jnp
from jax import lax
from jax.experimental import pallas as pl
from jax.experimental.pallas import tpu as pltpu
from jax.sharding import PartitionSpec as P

TAPS = 3
BLK = 256
TILE = 128
PAD = 8
GRANT = 24
START_GRANT = 60
MIB = 1 << 20


def params(mib):
    return pltpu.CompilerParams(vmem_limit_bytes=mib * MIB)


def short_filter(scr, taps_ref, which, keeps_ref, lanes):
    tok_rows = scr.shape[0] - 8
    total = taps_ref[0, which : which + 1, lanes] * scr[8 : 8 + tok_rows, lanes]
    for tap in range(1, TAPS):
        window = scr[8 - tap : 8 - tap + tok_rows, lanes] * keeps_ref[tap - 1]
        total = total + taps_ref[tap, which : which + 1, lanes] * window
    return total


def fill(scr, edge, values):
    scr[6:8, :] = edge.astype(jnp.float32)
    scr[8:, :] = values.astype(jnp.float32)


def fill_keeps(lengths_ref, keeps_ref):
    @pl.when(pl.program_id(0) == 0)
    def _():
        _, tok_rows, width = keeps_ref.shape
        place = lax.axis_index("seq") * tok_rows
        positions = place + lax.broadcasted_iota(jnp.int32, (tok_rows, width), 0)
        starts = jnp.zeros((tok_rows, width), jnp.int32)
        offset = jnp.int32(0)
        for prompt in range(lengths_ref.shape[0]):
            starts = jnp.where(positions >= offset, offset, starts)
            offset = offset + lengths_ref[prompt]
        for tap in range(1, TAPS):
            keeps_ref[tap - 1] = (positions - tap >= starts).astype(jnp.float32)


def lane_parts(width):
    return [slice(i, i + TILE) for i in range(0, width, TILE)]


def product_kernel(lengths_ref, k_ref, v_ref, edge_ref, taps_ref, out_ref, keeps_ref, scr_k, scr_v):
    fill_keeps(lengths_ref, keeps_ref)
    fill(scr_k, edge_ref[:, 1, :], k_ref[...])
    fill(scr_v, edge_ref[:, 2, :], v_ref[...])
    for lanes in lane_parts(k_ref.shape[1]):
        product = short_filter(scr_k, taps_ref, 1, keeps_ref, lanes) * short_filter(
            scr_v, taps_ref, 2, keeps_ref, lanes
        )
        out_ref[lanes, :] = product.T.astype(jnp.bfloat16)


def query_kernel(lengths_ref, q_ref, edge_ref, taps_ref, out_ref, keeps_ref, scr_q):
    fill_keeps(lengths_ref, keeps_ref)
    fill(scr_q, edge_ref[:, 0, :], q_ref[...])
    for lanes in lane_parts(q_ref.shape[1]):
        out_ref[:, lanes] = short_filter(scr_q, taps_ref, 0, keeps_ref, lanes).astype(jnp.bfloat16)


def short_call(kernel, lengths, by_kind, edge, taps, kinds, transposed, grant, width=512):
    _, tok_rows, channels = by_kind.shape
    if transposed:
        shape, spec = (channels, tok_rows), pl.BlockSpec((width, tok_rows), lambda i: (i, 0))
    else:
        shape, spec = (tok_rows, channels), pl.BlockSpec((tok_rows, width), lambda i: (0, i))
    return pl.pallas_call(
        kernel,
        grid=(channels // width,),
        out_shape=jax.ShapeDtypeStruct(shape, jnp.bfloat16),
        in_specs=[pl.BlockSpec(memory_space=pltpu.SMEM)]
        + [pl.BlockSpec((None, tok_rows, width), lambda i, kind=kind: (kind, 0, i)) for kind in kinds]
        + [
            pl.BlockSpec((TAPS - 1, 3, width), lambda i: (0, 0, i)),
            pl.BlockSpec((TAPS, 3, width), lambda i: (0, 0, i)),
        ],
        out_specs=spec,
        scratch_shapes=[pltpu.VMEM((TAPS - 1, tok_rows, TILE), jnp.float32)]
        + [pltpu.VMEM((tok_rows + 8, width), jnp.float32)] * len(kinds),
        compiler_params=params(grant),
        cost_estimate=pl.CostEstimate(flops=20 * tok_rows * channels, bytes_accessed=2 * MIB, transcendentals=0),
    )(lengths, *([by_kind] * len(kinds)), edge, taps)


def list_rows(lengths_ref, table, heads, rows):
    for row in range(rows - lengths_ref.shape[0], rows):
        for i in range(3):
            table[i, row] = jnp.int32(0)
    offset, row = jnp.int32(0), jnp.int32(0)
    for prompt in range(lengths_ref.shape[0]):
        end = offset + lengths_ref[prompt]
        first, last = offset // BLK, (end - 1) // BLK
        heads[1, prompt] = row

        def note(block, _, row=row, first=first, offset=offset, end=end):
            at = row + block - first
            table[0, at] = block
            table[1, at] = offset
            table[2, at] = end

            @pl.when(block * BLK >= offset)
            def _():
                heads[0, block] = at

            return 0

        lax.fori_loop(first, last + 1, note, 0)
        row = row + last - first + 1
        offset = end


def rows_before(lengths_ref, rows):
    row_ids = lax.broadcasted_iota(jnp.int32, (rows, TILE), 0)
    firsts = jnp.zeros((rows, TILE), jnp.int32)
    offset, row = jnp.int32(0), jnp.int32(0)
    for prompt in range(lengths_ref.shape[0]):
        firsts = jnp.where(row_ids >= row, row, firsts)
        end = offset + lengths_ref[prompt]
        row = row + (end - 1) // BLK - offset // BLK + 1
        offset = end
    return row_ids - firsts


def only_lanes(table, row, values, others):
    block, start, end = (table[i, row] for i in range(3))
    positions = block * BLK + lax.broadcasted_iota(jnp.int32, (8, BLK), 1)
    inside = (positions >= start) & (positions < end)
    shape = (values.shape[0] // 8, 8, BLK)
    others = others if isinstance(others, float) else others.reshape(shape)
    return jnp.where(inside[None], values.reshape(shape), others).reshape(values.shape)


def conv_kernel(lengths_ref, signal_ref, taps_ref, out_ref, table, heads, spread, result, before, toep, *, rows, rows_b):
    step = pl.program_id(0)
    devices, channels, _ = signal_ref.shape
    group, span = taps_ref.shape
    lags = span // BLK + 1
    tiles = span // TILE + 1
    pitch = PAD + rows_b

    @pl.when(step == 0)
    def _():
        list_rows(lengths_ref, table, heads, rows)
        for row in range(rows):
            slab = only_lanes(table, row, signal_ref[table[0, row]].astype(jnp.float32), 0.0)
            for h in range(2):
                spread[h, pl.ds(PAD + row, channels, stride=pitch), :] = slab[:, h * TILE : (h + 1) * TILE]
        before[...] = rows_before(lengths_ref, rows_b)

    views = spread.reshape(2, channels, pitch, TILE)
    zero = jnp.zeros((TILE, TILE), jnp.bfloat16)
    behind = before[...]

    def tile(g, t):
        return toep[g, t * TILE : (t + 1) * TILE, :] if 0 <= t < tiles else zero

    for g in range(group):
        channel = step * group + g
        row = jnp.concatenate([taps_ref[g : g + 1, :], jnp.zeros((1, TILE), jnp.float32)], 1)
        sheared = pltpu.roll(jnp.broadcast_to(row, (TILE, span + TILE)), 0, 1, stride=1, stride_axis=0)
        for t in range(tiles):
            toep[g, t * TILE : (t + 1) * TILE, :] = sheared[:, t * TILE : (t + 1) * TILE].astype(jnp.bfloat16)
        total = None
        for lag in range(lags):
            kept = behind >= lag
            left = jnp.concatenate(
                [
                    jnp.where(kept, views[h, channel, PAD - lag : PAD - lag + rows_b, :], 0.0).astype(jnp.bfloat16)
                    for h in range(2)
                ],
                1,
            )
            t = 2 * lag
            right = jnp.concatenate(
                [
                    jnp.concatenate([tile(g, t), tile(g, t + 1)], 1),
                    jnp.concatenate([tile(g, t - 1), tile(g, t)], 1),
                ],
                0,
            )
            term = jnp.dot(left, right, preferred_element_type=jnp.float32)
            total = term if total is None else total + term
        for h in range(2):
            result[h, pl.ds(channel * rows, rows), :] = total[:rows, h * TILE : (h + 1) * TILE]

    @pl.when(step == pl.num_programs(0) - 1)
    def _():
        def slab_of(row):
            return jnp.concatenate([result[h, pl.ds(row, channels, stride=rows), :] for h in range(2)], 1)

        for block in range(devices):
            out_ref[block] = slab_of(heads[0, block]).astype(jnp.bfloat16)
        for prompt in range(lengths_ref.shape[0]):
            row = heads[1, prompt]
            block = table[0, row]
            old = out_ref[block].astype(jnp.float32)
            out_ref[block] = only_lanes(table, row, slab_of(row), old).astype(jnp.bfloat16)


def long_conv(lengths, signal, taps, group=32):
    devices, channels, _ = signal.shape
    span = taps.shape[1]
    rows = -(-(devices + lengths.shape[0] - 1) // 8) * 8
    rows_b = -(-rows // 16) * 16
    return pl.pallas_call(
        functools.partial(conv_kernel, rows=rows, rows_b=rows_b),
        grid=(channels // group,),
        out_shape=jax.ShapeDtypeStruct(signal.shape, jnp.bfloat16),
        in_specs=[
            pl.BlockSpec(memory_space=pltpu.SMEM),
            pl.BlockSpec(signal.shape, lambda i: (0, 0, 0)),
            pl.BlockSpec((group, span), lambda i: (i, 0)),
        ],
        out_specs=pl.BlockSpec(signal.shape, lambda i: (0, 0, 0)),
        scratch_shapes=[
            pltpu.SMEM((3, rows), jnp.int32),
            pltpu.SMEM((2, devices), jnp.int32),
            pltpu.VMEM((2, channels * (PAD + rows_b), TILE), jnp.float32),
            pltpu.VMEM((2, channels * rows, TILE), jnp.float32),
            pltpu.VMEM((rows_b, TILE), jnp.int32),
            pltpu.VMEM((group, span + TILE, TILE), jnp.bfloat16),
        ],
        compiler_params=params(GRANT),
        cost_estimate=pl.CostEstimate(
            flops=2 * channels * rows * (span + BLK) * BLK, bytes_accessed=2 * MIB, transcendentals=0
        ),
    )(lengths, signal, taps)


def gate_kernel(query_ref, conv_ref, *out_refs):
    conv = conv_ref[...].astype(jnp.float32).T
    gated = (query_ref[...].astype(jnp.float32) * conv).astype(jnp.bfloat16)
    rows = gated.shape[0] // len(out_refs)
    for i, out_ref in enumerate(out_refs):
        out_ref[...] = gated[i * rows : (i + 1) * rows]


def gate(query, conv_t, pieces=2, width=256):
    tok_rows, channels = query.shape
    rows = tok_rows // pieces
    return pl.pallas_call(
        gate_kernel,
        grid=(channels // width,),
        out_shape=[jax.ShapeDtypeStruct((rows, channels), jnp.bfloat16)] * pieces,
        in_specs=[
            pl.BlockSpec((tok_rows, width), lambda i: (0, i)),
            pl.BlockSpec((width, tok_rows), lambda i: (i, 0)),
        ],
        out_specs=[pl.BlockSpec((rows, width), lambda i: (0, i))] * pieces,
        compiler_params=params(GRANT),
        cost_estimate=pl.CostEstimate(flops=tok_rows * channels, bytes_accessed=2 * MIB, transcendentals=0),
    )(query, conv_t)


def shift(array, axis, by):
    length = lax.axis_size(axis)
    return lax.ppermute(array, axis, [(i, (i + by) % length) for i in range(length)])


def project_kernel(*refs, count, pieces, has_total):
    blocks, weights = refs[: count * pieces], refs[count * pieces : count * (pieces + 1)]
    out_ref = refs[-1]
    total = refs[count * (pieces + 1)][...] if has_total else None
    for i in range(count):
        block = jnp.concatenate([ref[...] for ref in blocks[i * pieces : (i + 1) * pieces]], 0)
        term = jnp.dot(block, weights[i][...], preferred_element_type=jnp.float32)
        total = term if total is None else total + term
    out_ref[...] = total.astype(out_ref.dtype)


def project_part(blocks, weights, total, kind):
    count, pieces = len(blocks), len(blocks[0])
    rows, depth = blocks[0][0].shape
    columns = weights[0].shape[1]
    tok_rows = rows * pieces
    operands = [piece for block in blocks for piece in block] + weights + ([] if total is None else [total])
    return pl.pallas_call(
        functools.partial(project_kernel, count=count, pieces=pieces, has_total=total is not None),
        out_shape=jax.ShapeDtypeStruct((tok_rows, columns), kind),
        compiler_params=params(GRANT),
        cost_estimate=pl.CostEstimate(
            flops=2 * count * tok_rows * depth * columns,
            bytes_accessed=2 * count * depth * columns,
            transcendentals=0,
        ),
    )(*operands)


def project(pieces, w_out):
    size = lax.axis_size("ch")
    place = lax.axis_index("ch")
    depth = pieces[0].shape[1]
    own, after, far_rows, before = (
        lax.dynamic_slice_in_dim(w_out, (place + i) % size * depth, depth, 0) for i in range(size)
    )
    up, down = pieces
    right_up, left_down = shift(up, "ch", 1), shift(down, "ch", -1)
    right_down, left_up = shift(down, "ch", 1), shift(up, "ch", -1)
    far_up, far_down = shift(right_up, "ch", 1), shift(left_down, "ch", -1)
    total = project_part([(up, down)], [own], None, jnp.float32)
    near = [(right_up, right_down), (left_up, left_down)]
    total = project_part(near, [before, after], total, jnp.float32)
    return project_part([(far_up, far_down)], [far_rows], total, jnp.bfloat16)


def per_device(qkv, short_taps, lengths, filter_taps, w_out):
    tok_rows, _, width = qkv.shape
    lead = TAPS - 1
    seq = lax.axis_size("seq")
    edge = lax.ppermute(qkv[tok_rows - lead :], "seq", [(i, i + 1) for i in range(seq - 1)])
    by_kind = qkv.transpose(1, 0, 2)
    product_t = short_call(product_kernel, lengths, by_kind, edge, short_taps, (1, 2), True, START_GRANT)
    query = short_call(query_kernel, lengths, by_kind, edge, short_taps, (0,), False, GRANT)
    signal = lax.all_to_all(product_t.reshape(seq, width // seq, tok_rows), "seq", 0, 0, tiled=True)
    conv = long_conv(lengths, signal, filter_taps[0])
    conv_t = lax.all_to_all(conv, "seq", 0, 0, tiled=True).reshape(width, tok_rows)
    return project(gate(query, conv_t), w_out)


def solution(mesh):
    placed = (P("seq", None, "ch"), P(None, None, "ch"), P(), P("ch", "seq", None), P(None, "ch"))
    return jax.shard_map(
        per_device, mesh=mesh, in_specs=placed, out_specs=P("seq", "ch"), check_vma=False
    )
```

```python
import functools

import jax
import jax.numpy as jnp
from jax import lax
from jax.experimental import pallas as pl
from jax.experimental.pallas import tpu as pltpu
from jax.sharding import PartitionSpec as P

TAPS = 3
BLK = 256
TILE = 128
PAD = 8
GRANT = 24
START_GRANT = 60
EDGES = 8
MIB = 1 << 20


def params(mib):
    return pltpu.CompilerParams(vmem_limit_bytes=mib * MIB)


def short_filter(scr, taps_ref, which, keeps_ref, lanes):
    tok_rows = scr.shape[0] - 8
    total = taps_ref[0, which : which + 1, lanes] * scr[8 : 8 + tok_rows, lanes]
    for tap in range(1, TAPS):
        window = scr[8 - tap : 8 - tap + tok_rows, lanes] * keeps_ref[tap - 1]
        total = total + taps_ref[tap, which : which + 1, lanes] * window
    return total


def fill(scr, values, edge=None):
    scr[:8, :] = jnp.zeros((8, scr.shape[1]), jnp.float32)
    if edge is not None:
        scr[6:8, :] = edge.astype(jnp.float32)
    scr[8:, :] = values.astype(jnp.float32)


def fill_keeps(lengths_ref, keeps_ref):
    @pl.when(pl.program_id(0) == 0)
    def _():
        _, tok_rows, width = keeps_ref.shape
        place = lax.axis_index("seq") * tok_rows
        positions = place + lax.broadcasted_iota(jnp.int32, (tok_rows, width), 0)
        starts = jnp.zeros((tok_rows, width), jnp.int32)
        offset = jnp.int32(0)
        for prompt in range(lengths_ref.shape[0]):
            starts = jnp.where(positions >= offset, offset, starts)
            offset = offset + lengths_ref[prompt]
        for tap in range(1, TAPS):
            keeps_ref[tap - 1] = (positions - tap >= starts).astype(jnp.float32)


def lane_parts(width):
    return [slice(i, i + TILE) for i in range(0, width, TILE)]


def product_kernel(lengths_ref, k_ref, v_ref, taps_ref, out_ref, keeps_ref, scr_k, scr_v):
    fill_keeps(lengths_ref, keeps_ref)
    fill(scr_k, k_ref[...])
    fill(scr_v, v_ref[...])
    held = out_ref.shape[1] - EDGES
    tok_rows, width = k_ref.shape
    for lanes in lane_parts(width):
        product = short_filter(scr_k, taps_ref, 1, keeps_ref, lanes) * short_filter(
            scr_v, taps_ref, 2, keeps_ref, lanes
        )
        product = product.T
        outer = [scr[8 + t : 10 + t, lanes] for scr in (scr_k, scr_v) for t in (0, tok_rows - 2)]
        outer = jnp.concatenate(outer, 0)
        for i in range(TILE // held):
            mine = outer if i == 0 else pltpu.roll(outer, TILE - i * held, 1)
            mine = jnp.concatenate([mine, jnp.zeros((EDGES, tok_rows - TILE), jnp.float32)], 1)
            rows = jnp.concatenate([product[i * held : (i + 1) * held], mine], 0)
            out_ref[lanes.start // held + i] = rows.astype(jnp.bfloat16)


def query_kernel(lengths_ref, q_ref, edge_ref, taps_ref, out_ref, keeps_ref, scr_q):
    fill_keeps(lengths_ref, keeps_ref)
    fill(scr_q, q_ref[...], edge_ref[...])
    for lanes in lane_parts(q_ref.shape[1]):
        out_ref[:, lanes] = short_filter(scr_q, taps_ref, 0, keeps_ref, lanes).astype(jnp.bfloat16)


def short_call(kernel, lengths, by_kind, edge, taps, kinds, shape, block, grant, width=512):
    _, tok_rows, channels = by_kind.shape
    steps = channels // width
    return pl.pallas_call(
        kernel,
        grid=(steps,),
        out_shape=jax.ShapeDtypeStruct(shape, jnp.bfloat16),
        in_specs=[pl.BlockSpec(memory_space=pltpu.SMEM)]
        + [pl.BlockSpec((None, tok_rows, width), lambda i, kind=kind: (kind, 0, i)) for kind in kinds]
        + [pl.BlockSpec((TAPS - 1, width), lambda i: (0, i))] * (edge is not None)
        + [pl.BlockSpec((TAPS, 3, width), lambda i: (0, 0, i))],
        out_specs=block,
        scratch_shapes=[pltpu.VMEM((TAPS - 1, tok_rows, TILE), jnp.float32)]
        + [pltpu.VMEM((tok_rows + 8, width), jnp.float32)] * len(kinds),
        compiler_params=params(grant),
        cost_estimate=pl.CostEstimate(flops=20 * tok_rows * channels, bytes_accessed=2 * MIB, transcendentals=0),
    )(lengths, *([by_kind] * len(kinds)), *([] if edge is None else [edge]), taps)


def products(lengths, by_kind, taps, devices, width=512):
    _, tok_rows, channels = by_kind.shape
    held = channels // devices
    shape = (devices, held + EDGES, tok_rows)
    block = pl.BlockSpec((width // held,) + shape[1:], lambda i: (i, 0, 0))
    return short_call(product_kernel, lengths, by_kind, None, taps, (1, 2), shape, block, START_GRANT, width)


def queries(lengths, by_kind, edge, taps, width=512):
    _, tok_rows, channels = by_kind.shape
    block = pl.BlockSpec((tok_rows, width), lambda i: (0, i))
    return short_call(query_kernel, lengths, by_kind, edge, taps, (0,), (tok_rows, channels), block, GRANT, width)


def list_rows(lengths_ref, table, heads, rows):
    for row in range(rows - lengths_ref.shape[0], rows):
        for i in range(3):
            table[i, row] = jnp.int32(0)
    offset, row = jnp.int32(0), jnp.int32(0)
    for prompt in range(lengths_ref.shape[0]):
        end = offset + lengths_ref[prompt]
        first, last = offset // BLK, (end - 1) // BLK
        heads[1, prompt] = row

        def note(block, _, row=row, first=first, offset=offset, end=end):
            at = row + block - first
            table[0, at] = block
            table[1, at] = offset
            table[2, at] = end

            @pl.when(block * BLK >= offset)
            def _():
                heads[0, block] = at

            return 0

        lax.fori_loop(first, last + 1, note, 0)
        row = row + last - first + 1
        offset = end


def rows_before(lengths_ref, rows):
    row_ids = lax.broadcasted_iota(jnp.int32, (rows, TILE), 0)
    firsts = jnp.zeros((rows, TILE), jnp.int32)
    offset, row = jnp.int32(0), jnp.int32(0)
    for prompt in range(lengths_ref.shape[0]):
        firsts = jnp.where(row_ids >= row, row, firsts)
        end = offset + lengths_ref[prompt]
        row = row + (end - 1) // BLK - offset // BLK + 1
        offset = end
    return row_ids - firsts


def only_lanes(table, row, values, others):
    block, start, end = (table[i, row] for i in range(3))
    positions = block * BLK + lax.broadcasted_iota(jnp.int32, (8, BLK), 1)
    inside = (positions >= start) & (positions < end)
    shape = (values.shape[0] // 8, 8, BLK)
    others = others if isinstance(others, float) else others.reshape(shape)
    return jnp.where(inside[None], values.reshape(shape), others).reshape(values.shape)


def first_products(lengths_ref, edges, short_ref, channels):
    count = edges.shape[0]
    place = lax.axis_index("seq") * channels
    here = pl.ds(pl.multiple_of(place // TILE * TILE, TILE), TILE)
    rows = [short_ref[tap, which : which + 1, here] for which in (1, 2) for tap in range(TAPS)]
    rows = jnp.concatenate(rows + [jnp.zeros((2, TILE), jnp.float32)], 0)
    rows = pltpu.roll(rows, TILE - place % TILE, 1)
    columns = jnp.concatenate([rows, jnp.zeros((TILE - 8, TILE), jnp.float32)], 0).T[:channels]
    own = edges.T[:channels]
    lane = lax.broadcasted_iota(jnp.int32, (channels, count), 1)
    positions = lane // EDGES * BLK + lane % EDGES
    starts = jnp.zeros((channels, count), jnp.int32)
    offset = jnp.int32(0)
    for prompt in range(lengths_ref.shape[0]):
        starts = jnp.where(positions >= offset, offset, starts)
        offset = offset + lengths_ref[prompt]
    product = None
    for i in range(2):
        now = own if i == 0 else pltpu.roll(own, count - 4, 1)
        one = jnp.where(lane % EDGES == 0, pltpu.roll(now, 5, 1), pltpu.roll(now, 1, 1))
        two = pltpu.roll(now, 6, 1)
        total = columns[:, 3 * i : 3 * i + 1] * now
        for tap, value in ((1, one), (2, two)):
            keep = (positions - tap >= starts).astype(jnp.float32)
            total = total + columns[:, 3 * i + tap : 3 * i + tap + 1] * (value * keep)
        product = total if product is None else product * total
    return product.astype(jnp.bfloat16).astype(jnp.float32)


def conv_kernel(
    lengths_ref, signal_ref, taps_ref, short_ref, out_ref, table, heads, blocks, edges, spread, result, before, toep, *, rows, rows_b
):
    step = pl.program_id(0)
    devices, channels, _ = out_ref.shape
    group, span = taps_ref.shape
    lags = span // BLK + 1
    tiles = span // TILE + 1
    pitch = PAD + rows_b

    @pl.when(step == 0)
    def _():
        list_rows(lengths_ref, table, heads, rows)
        for device in range(devices):
            arrived = signal_ref[device].astype(jnp.float32)
            blocks[device] = arrived[:channels]
            edges[device * EDGES : (device + 1) * EDGES, :] = arrived[channels:, :TILE]
        firsts = first_products(lengths_ref, edges[...], short_ref, channels)
        is_first = lax.broadcasted_iota(jnp.int32, (channels, TILE), 1) < TAPS - 1
        for device in range(devices):
            at = device * EDGES
            mine = firsts[:, at // TILE * TILE : (at // TILE + 1) * TILE]
            mine = mine if at % TILE == 0 else pltpu.roll(mine, TILE - at % TILE, 1)
            blocks[device, :, :TILE] = jnp.where(is_first, mine, blocks[device, :, :TILE])
        for row in range(rows):
            slab = only_lanes(table, row, blocks[table[0, row]], 0.0)
            for h in range(2):
                spread[h, pl.ds(PAD + row, channels, stride=pitch), :] = slab[:, h * TILE : (h + 1) * TILE]
        before[...] = rows_before(lengths_ref, rows_b)

    views = spread.reshape(2, channels, pitch, TILE)
    zero = jnp.zeros((TILE, TILE), jnp.bfloat16)
    behind = before[...]

    def tile(g, t):
        return toep[g, t * TILE : (t + 1) * TILE, :] if 0 <= t < tiles else zero

    for g in range(group):
        channel = step * group + g
        row = jnp.concatenate([taps_ref[g : g + 1, :], jnp.zeros((1, TILE), jnp.float32)], 1)
        sheared = pltpu.roll(jnp.broadcast_to(row, (TILE, span + TILE)), 0, 1, stride=1, stride_axis=0)
        for t in range(tiles):
            toep[g, t * TILE : (t + 1) * TILE, :] = sheared[:, t * TILE : (t + 1) * TILE].astype(jnp.bfloat16)
        total = None
        for lag in range(lags):
            kept = behind >= lag
            left = jnp.concatenate(
                [
                    jnp.where(kept, views[h, channel, PAD - lag : PAD - lag + rows_b, :], 0.0).astype(jnp.bfloat16)
                    for h in range(2)
                ],
                1,
            )
            t = 2 * lag
            right = jnp.concatenate(
                [
                    jnp.concatenate([tile(g, t), tile(g, t + 1)], 1),
                    jnp.concatenate([tile(g, t - 1), tile(g, t)], 1),
                ],
                0,
            )
            term = jnp.dot(left, right, preferred_element_type=jnp.float32)
            total = term if total is None else total + term
        for h in range(2):
            result[h, pl.ds(channel * rows, rows), :] = total[:rows, h * TILE : (h + 1) * TILE]

    @pl.when(step == pl.num_programs(0) - 1)
    def _():
        def slab_of(row):
            return jnp.concatenate([result[h, pl.ds(row, channels, stride=rows), :] for h in range(2)], 1)

        for block in range(devices):
            out_ref[block] = slab_of(heads[0, block]).astype(jnp.bfloat16)
        for prompt in range(lengths_ref.shape[0]):
            row = heads[1, prompt]
            block = table[0, row]
            old = out_ref[block].astype(jnp.float32)
            out_ref[block] = only_lanes(table, row, slab_of(row), old).astype(jnp.bfloat16)


def long_conv(lengths, signal, taps, short_taps, group=32):
    devices, _, tok_rows = signal.shape
    channels = taps.shape[0]
    shape = (devices, channels, tok_rows)
    span = taps.shape[1]
    rows = -(-(devices + lengths.shape[0] - 1) // 8) * 8
    rows_b = -(-rows // 16) * 16
    return pl.pallas_call(
        functools.partial(conv_kernel, rows=rows, rows_b=rows_b),
        grid=(channels // group,),
        out_shape=jax.ShapeDtypeStruct(shape, jnp.bfloat16),
        in_specs=[
            pl.BlockSpec(memory_space=pltpu.SMEM),
            pl.BlockSpec(signal.shape, lambda i: (0, 0, 0)),
            pl.BlockSpec((group, span), lambda i: (i, 0)),
            pl.BlockSpec(short_taps.shape, lambda i: (0, 0, 0)),
        ],
        out_specs=pl.BlockSpec(shape, lambda i: (0, 0, 0)),
        scratch_shapes=[
            pltpu.SMEM((3, rows), jnp.int32),
            pltpu.SMEM((2, devices), jnp.int32),
            pltpu.VMEM(shape, jnp.float32),
            pltpu.VMEM((devices * EDGES, TILE), jnp.float32),
            pltpu.VMEM((2, channels * (PAD + rows_b), TILE), jnp.float32),
            pltpu.VMEM((2, channels * rows, TILE), jnp.float32),
            pltpu.VMEM((rows_b, TILE), jnp.int32),
            pltpu.VMEM((group, span + TILE, TILE), jnp.bfloat16),
        ],
        compiler_params=params(GRANT),
        cost_estimate=pl.CostEstimate(
            flops=2 * channels * rows * (span + BLK) * BLK, bytes_accessed=2 * MIB, transcendentals=0
        ),
    )(lengths, signal, taps, short_taps)


def gate_kernel(query_ref, conv_ref, *out_refs):
    conv = conv_ref[...].astype(jnp.float32).T
    gated = (query_ref[...].astype(jnp.float32) * conv).astype(jnp.bfloat16)
    rows = gated.shape[0] // len(out_refs)
    for i, out_ref in enumerate(out_refs):
        out_ref[...] = gated[i * rows : (i + 1) * rows]


def gate(query, conv_t, pieces=2, width=256):
    tok_rows, channels = query.shape
    rows = tok_rows // pieces
    return pl.pallas_call(
        gate_kernel,
        grid=(channels // width,),
        out_shape=[jax.ShapeDtypeStruct((rows, channels), jnp.bfloat16)] * pieces,
        in_specs=[
            pl.BlockSpec((tok_rows, width), lambda i: (0, i)),
            pl.BlockSpec((width, tok_rows), lambda i: (i, 0)),
        ],
        out_specs=[pl.BlockSpec((rows, width), lambda i: (0, i))] * pieces,
        compiler_params=params(GRANT),
        cost_estimate=pl.CostEstimate(flops=tok_rows * channels, bytes_accessed=2 * MIB, transcendentals=0),
    )(query, conv_t)


def shift(array, axis, by):
    length = lax.axis_size(axis)
    return lax.ppermute(array, axis, [(i, (i + by) % length) for i in range(length)])


def project_kernel(*refs, count, pieces, has_total):
    blocks, weights = refs[: count * pieces], refs[count * pieces : count * (pieces + 1)]
    out_ref = refs[-1]
    total = refs[count * (pieces + 1)][...] if has_total else None
    for i in range(count):
        block = jnp.concatenate([ref[...] for ref in blocks[i * pieces : (i + 1) * pieces]], 0)
        term = jnp.dot(block, weights[i][...], preferred_element_type=jnp.float32)
        total = term if total is None else total + term
    out_ref[...] = total.astype(out_ref.dtype)


def project_part(blocks, weights, total, kind):
    count, pieces = len(blocks), len(blocks[0])
    rows, depth = blocks[0][0].shape
    columns = weights[0].shape[1]
    tok_rows = rows * pieces
    operands = [piece for block in blocks for piece in block] + weights + ([] if total is None else [total])
    return pl.pallas_call(
        functools.partial(project_kernel, count=count, pieces=pieces, has_total=total is not None),
        out_shape=jax.ShapeDtypeStruct((tok_rows, columns), kind),
        compiler_params=params(GRANT),
        cost_estimate=pl.CostEstimate(
            flops=2 * count * tok_rows * depth * columns,
            bytes_accessed=2 * count * depth * columns,
            transcendentals=0,
        ),
    )(*operands)


def project(pieces, w_out):
    size = lax.axis_size("ch")
    place = lax.axis_index("ch")
    depth = pieces[0].shape[1]
    own, after, far_rows, before = (
        lax.dynamic_slice_in_dim(w_out, (place + i) % size * depth, depth, 0) for i in range(size)
    )
    up, down = pieces
    right_up, left_down = shift(up, "ch", 1), shift(down, "ch", -1)
    right_down, left_up = shift(down, "ch", 1), shift(up, "ch", -1)
    far_up, far_down = shift(right_up, "ch", 1), shift(left_down, "ch", -1)
    total = project_part([(up, down)], [own], None, jnp.float32)
    near = [(right_up, right_down), (left_up, left_down)]
    total = project_part(near, [before, after], total, jnp.float32)
    return project_part([(far_up, far_down)], [far_rows], total, jnp.bfloat16)


def per_device(qkv, short_taps, lengths, filter_taps, w_out):
    tok_rows, _, width = qkv.shape
    lead = TAPS - 1
    seq = lax.axis_size("seq")
    by_kind = qkv.transpose(1, 0, 2)
    sent = products(lengths, by_kind, short_taps, seq)
    signal = lax.all_to_all(sent, "seq", 0, 0, tiled=True)
    conv = long_conv(lengths, signal, filter_taps[0], short_taps)
    late, conv = lax.optimization_barrier((by_kind, conv))
    edge = lax.ppermute(late[0, tok_rows - lead :], "seq", [(i, i + 1) for i in range(seq - 1)])
    query = queries(lengths, late, edge, short_taps)
    conv_t = lax.all_to_all(conv, "seq", 0, 0, tiled=True).reshape(width, tok_rows)
    return project(gate(query, conv_t), w_out)


def solution(mesh):
    placed = (P("seq", None, "ch"), P(None, None, "ch"), P(), P("ch", "seq", None), P(None, "ch"))
    return jax.shard_map(
        per_device, mesh=mesh, in_specs=placed, out_specs=P("seq", "ch"), check_vma=False
    )
```

```python
import functools

import jax
import jax.numpy as jnp
from jax import lax
from jax.experimental import pallas as pl
from jax.experimental.pallas import tpu as pltpu
from jax.sharding import PartitionSpec as P

TAPS = 3
BLK = 256
TILE = 128
PAD = 8
GRANT = 24
START_GRANT = 60
EDGES = 8
MIB = 1 << 20


def params(mib):
    return pltpu.CompilerParams(vmem_limit_bytes=mib * MIB)


def short_filter(scr, taps_ref, which, keeps_ref, lanes):
    tok_rows = scr.shape[0] - 8
    total = taps_ref[0, which : which + 1, lanes] * scr[8 : 8 + tok_rows, lanes]
    for tap in range(1, TAPS):
        window = scr[8 - tap : 8 - tap + tok_rows, lanes] * keeps_ref[tap - 1]
        total = total + taps_ref[tap, which : which + 1, lanes] * window
    return total


def fill(scr, values, edge=None):
    scr[:8, :] = jnp.zeros((8, scr.shape[1]), jnp.float32)
    if edge is not None:
        scr[6:8, :] = edge.astype(jnp.float32)
    scr[8:, :] = values.astype(jnp.float32)


def fill_keeps(lengths_ref, keeps_ref):
    @pl.when(pl.program_id(0) == 0)
    def _():
        _, tok_rows, width = keeps_ref.shape
        place = lax.axis_index("seq") * tok_rows
        positions = place + lax.broadcasted_iota(jnp.int32, (tok_rows, width), 0)
        starts = jnp.zeros((tok_rows, width), jnp.int32)
        offset = jnp.int32(0)
        for prompt in range(lengths_ref.shape[0]):
            starts = jnp.where(positions >= offset, offset, starts)
            offset = offset + lengths_ref[prompt]
        for tap in range(1, TAPS):
            keeps_ref[tap - 1] = (positions - tap >= starts).astype(jnp.float32)


def lane_parts(width):
    return [slice(i, i + TILE) for i in range(0, width, TILE)]


def product_kernel(lengths_ref, k_ref, v_ref, taps_ref, out_ref, keeps_ref, scr_k, scr_v):
    fill_keeps(lengths_ref, keeps_ref)
    fill(scr_k, k_ref[...])
    fill(scr_v, v_ref[...])
    tok_rows, width = k_ref.shape
    held = (out_ref.shape[1] - EDGES) * TILE // tok_rows
    for lanes in lane_parts(width):
        product = short_filter(scr_k, taps_ref, 1, keeps_ref, lanes) * short_filter(
            scr_v, taps_ref, 2, keeps_ref, lanes
        )
        product = product.T
        halves = [product[:, at : at + TILE] for at in range(0, tok_rows, TILE)]
        outer = [scr[8 + t : 10 + t, lanes] for scr in (scr_k, scr_v) for t in (0, tok_rows - 2)]
        outer = jnp.concatenate(outer, 0)
        for i in range(TILE // held):
            mine = outer if i == 0 else pltpu.roll(outer, TILE - i * held, 1)
            rows = jnp.concatenate([half[i * held : (i + 1) * held] for half in halves] + [mine], 0)
            out_ref[lanes.start // held + i] = rows.astype(jnp.bfloat16)


def query_kernel(lengths_ref, q_ref, edge_ref, taps_ref, out_ref, keeps_ref, scr_q):
    fill_keeps(lengths_ref, keeps_ref)
    fill(scr_q, q_ref[...], edge_ref[...])
    for lanes in lane_parts(q_ref.shape[1]):
        out_ref[:, lanes] = short_filter(scr_q, taps_ref, 0, keeps_ref, lanes).astype(jnp.bfloat16)


def short_call(kernel, lengths, by_kind, edge, taps, kinds, shape, block, grant, width=512):
    _, tok_rows, channels = by_kind.shape
    steps = channels // width
    return pl.pallas_call(
        kernel,
        grid=(steps,),
        out_shape=jax.ShapeDtypeStruct(shape, jnp.bfloat16),
        in_specs=[pl.BlockSpec(memory_space=pltpu.SMEM)]
        + [pl.BlockSpec((None, tok_rows, width), lambda i, kind=kind: (kind, 0, i)) for kind in kinds]
        + [pl.BlockSpec((TAPS - 1, width), lambda i: (0, i))] * (edge is not None)
        + [pl.BlockSpec((TAPS, 3, width), lambda i: (0, 0, i))],
        out_specs=block,
        scratch_shapes=[pltpu.VMEM((TAPS - 1, tok_rows, TILE), jnp.float32)]
        + [pltpu.VMEM((tok_rows + 8, width), jnp.float32)] * len(kinds),
        compiler_params=params(grant),
        cost_estimate=pl.CostEstimate(flops=20 * tok_rows * channels, bytes_accessed=2 * MIB, transcendentals=0),
    )(lengths, *([by_kind] * len(kinds)), *([] if edge is None else [edge]), taps)


def products(lengths, by_kind, taps, devices, width=512):
    _, tok_rows, channels = by_kind.shape
    held = channels // devices
    shape = (devices, held * tok_rows // TILE + EDGES, TILE)
    block = pl.BlockSpec((width // held,) + shape[1:], lambda i: (i, 0, 0))
    return short_call(product_kernel, lengths, by_kind, None, taps, (1, 2), shape, block, START_GRANT, width)


def queries(lengths, by_kind, edge, taps, width=512):
    _, tok_rows, channels = by_kind.shape
    block = pl.BlockSpec((tok_rows, width), lambda i: (0, i))
    return short_call(query_kernel, lengths, by_kind, edge, taps, (0,), (tok_rows, channels), block, GRANT, width)


def list_rows(lengths_ref, table, heads, rows):
    for row in range(rows - lengths_ref.shape[0], rows):
        for i in range(3):
            table[i, row] = jnp.int32(0)
    offset, row = jnp.int32(0), jnp.int32(0)
    for prompt in range(lengths_ref.shape[0]):
        end = offset + lengths_ref[prompt]
        first, last = offset // BLK, (end - 1) // BLK
        heads[1, prompt] = row

        def note(block, _, row=row, first=first, offset=offset, end=end):
            at = row + block - first
            table[0, at] = block
            table[1, at] = offset
            table[2, at] = end

            @pl.when(block * BLK >= offset)
            def _():
                heads[0, block] = at

            return 0

        lax.fori_loop(first, last + 1, note, 0)
        row = row + last - first + 1
        offset = end


def rows_before(lengths_ref, rows):
    row_ids = lax.broadcasted_iota(jnp.int32, (rows, TILE), 0)
    firsts = jnp.zeros((rows, TILE), jnp.int32)
    offset, row = jnp.int32(0), jnp.int32(0)
    for prompt in range(lengths_ref.shape[0]):
        firsts = jnp.where(row_ids >= row, row, firsts)
        end = offset + lengths_ref[prompt]
        row = row + (end - 1) // BLK - offset // BLK + 1
        offset = end
    return row_ids - firsts


def only_lanes(table, row, values, others):
    block, start, end = (table[i, row] for i in range(3))
    positions = block * BLK + lax.broadcasted_iota(jnp.int32, (8, BLK), 1)
    inside = (positions >= start) & (positions < end)
    shape = (values.shape[0] // 8, 8, BLK)
    others = others if isinstance(others, float) else others.reshape(shape)
    return jnp.where(inside[None], values.reshape(shape), others).reshape(values.shape)


def first_products(lengths_ref, edges, short_ref, channels):
    count = edges.shape[0]
    place = lax.axis_index("seq") * channels
    here = pl.ds(pl.multiple_of(place // TILE * TILE, TILE), TILE)
    rows = [short_ref[tap, which : which + 1, here] for which in (1, 2) for tap in range(TAPS)]
    rows = jnp.concatenate(rows + [jnp.zeros((2, TILE), jnp.float32)], 0)
    rows = pltpu.roll(rows, TILE - place % TILE, 1)
    columns = jnp.concatenate([rows, jnp.zeros((TILE - 8, TILE), jnp.float32)], 0).T[:channels]
    own = edges.T[:channels]
    lane = lax.broadcasted_iota(jnp.int32, (channels, count), 1)
    positions = lane // EDGES * BLK + lane % EDGES
    starts = jnp.zeros((channels, count), jnp.int32)
    offset = jnp.int32(0)
    for prompt in range(lengths_ref.shape[0]):
        starts = jnp.where(positions >= offset, offset, starts)
        offset = offset + lengths_ref[prompt]
    product = None
    for i in range(2):
        now = own if i == 0 else pltpu.roll(own, count - 4, 1)
        one = jnp.where(lane % EDGES == 0, pltpu.roll(now, 5, 1), pltpu.roll(now, 1, 1))
        two = pltpu.roll(now, 6, 1)
        total = columns[:, 3 * i : 3 * i + 1] * now
        for tap, value in ((1, one), (2, two)):
            keep = (positions - tap >= starts).astype(jnp.float32)
            total = total + columns[:, 3 * i + tap : 3 * i + tap + 1] * (value * keep)
        product = total if product is None else product * total
    return product.astype(jnp.bfloat16).astype(jnp.float32)


def conv_kernel(
    lengths_ref, signal_ref, taps_ref, short_ref, out_ref, table, heads, blocks, edges, spread, result, before, toep, *, rows, rows_b
):
    step = pl.program_id(0)
    devices, channels, _ = out_ref.shape
    group, span = taps_ref.shape
    lags = span // BLK + 1
    tiles = span // TILE + 1
    pitch = PAD + rows_b

    @pl.when(step == 0)
    def _():
        list_rows(lengths_ref, table, heads, rows)
        for device in range(devices):
            arrived = signal_ref[device].astype(jnp.float32)
            for h in range(2):
                blocks[device, :, h * TILE : (h + 1) * TILE] = arrived[h * channels : (h + 1) * channels]
            edges[device * EDGES : (device + 1) * EDGES, :] = arrived[2 * channels :]
        firsts = first_products(lengths_ref, edges[...], short_ref, channels)
        is_first = lax.broadcasted_iota(jnp.int32, (channels, TILE), 1) < TAPS - 1
        for device in range(devices):
            at = device * EDGES
            mine = firsts[:, at // TILE * TILE : (at // TILE + 1) * TILE]
            mine = mine if at % TILE == 0 else pltpu.roll(mine, TILE - at % TILE, 1)
            blocks[device, :, :TILE] = jnp.where(is_first, mine, blocks[device, :, :TILE])
        for row in range(rows):
            slab = only_lanes(table, row, blocks[table[0, row]], 0.0)
            for h in range(2):
                spread[h, pl.ds(PAD + row, channels, stride=pitch), :] = slab[:, h * TILE : (h + 1) * TILE]
        before[...] = rows_before(lengths_ref, rows_b)

    views = spread.reshape(2, channels, pitch, TILE)
    zero = jnp.zeros((TILE, TILE), jnp.bfloat16)
    behind = before[...]

    def tile(g, t):
        return toep[g, t * TILE : (t + 1) * TILE, :] if 0 <= t < tiles else zero

    for g in range(group):
        channel = step * group + g
        row = jnp.concatenate([taps_ref[g : g + 1, :], jnp.zeros((1, TILE), jnp.float32)], 1)
        sheared = pltpu.roll(jnp.broadcast_to(row, (TILE, span + TILE)), 0, 1, stride=1, stride_axis=0)
        for t in range(tiles):
            toep[g, t * TILE : (t + 1) * TILE, :] = sheared[:, t * TILE : (t + 1) * TILE].astype(jnp.bfloat16)
        total = None
        for lag in range(lags):
            kept = behind >= lag
            left = jnp.concatenate(
                [
                    jnp.where(kept, views[h, channel, PAD - lag : PAD - lag + rows_b, :], 0.0).astype(jnp.bfloat16)
                    for h in range(2)
                ],
                1,
            )
            t = 2 * lag
            right = jnp.concatenate(
                [
                    jnp.concatenate([tile(g, t), tile(g, t + 1)], 1),
                    jnp.concatenate([tile(g, t - 1), tile(g, t)], 1),
                ],
                0,
            )
            term = jnp.dot(left, right, preferred_element_type=jnp.float32)
            total = term if total is None else total + term
        for h in range(2):
            result[h, pl.ds(channel * rows, rows), :] = total[:rows, h * TILE : (h + 1) * TILE]

    @pl.when(step == pl.num_programs(0) - 1)
    def _():
        def slab_of(row):
            return jnp.concatenate([result[h, pl.ds(row, channels, stride=rows), :] for h in range(2)], 1)

        for block in range(devices):
            out_ref[block] = slab_of(heads[0, block]).astype(jnp.bfloat16)
        for prompt in range(lengths_ref.shape[0]):
            row = heads[1, prompt]
            block = table[0, row]
            old = out_ref[block].astype(jnp.float32)
            out_ref[block] = only_lanes(table, row, slab_of(row), old).astype(jnp.bfloat16)


def long_conv(lengths, signal, taps, short_taps, group=32):
    devices, tok_rows = signal.shape[0], BLK
    channels = taps.shape[0]
    shape = (devices, channels, tok_rows)
    span = taps.shape[1]
    rows = -(-(devices + lengths.shape[0] - 1) // 8) * 8
    rows_b = -(-rows // 16) * 16
    return pl.pallas_call(
        functools.partial(conv_kernel, rows=rows, rows_b=rows_b),
        grid=(channels // group,),
        out_shape=jax.ShapeDtypeStruct(shape, jnp.bfloat16),
        in_specs=[
            pl.BlockSpec(memory_space=pltpu.SMEM),
            pl.BlockSpec(signal.shape, lambda i: (0, 0, 0)),
            pl.BlockSpec((group, span), lambda i: (i, 0)),
            pl.BlockSpec(short_taps.shape, lambda i: (0, 0, 0)),
        ],
        out_specs=pl.BlockSpec(shape, lambda i: (0, 0, 0)),
        scratch_shapes=[
            pltpu.SMEM((3, rows), jnp.int32),
            pltpu.SMEM((2, devices), jnp.int32),
            pltpu.VMEM(shape, jnp.float32),
            pltpu.VMEM((devices * EDGES, TILE), jnp.float32),
            pltpu.VMEM((2, channels * (PAD + rows_b), TILE), jnp.float32),
            pltpu.VMEM((2, channels * rows, TILE), jnp.float32),
            pltpu.VMEM((rows_b, TILE), jnp.int32),
            pltpu.VMEM((group, span + TILE, TILE), jnp.bfloat16),
        ],
        compiler_params=params(GRANT),
        cost_estimate=pl.CostEstimate(
            flops=2 * channels * rows * (span + BLK) * BLK, bytes_accessed=2 * MIB, transcendentals=0
        ),
    )(lengths, signal, taps, short_taps)


def gate_kernel(query_ref, conv_ref, *out_refs):
    conv = conv_ref[...].astype(jnp.float32).T
    gated = (query_ref[...].astype(jnp.float32) * conv).astype(jnp.bfloat16)
    rows = gated.shape[0] // len(out_refs)
    for i, out_ref in enumerate(out_refs):
        out_ref[...] = gated[i * rows : (i + 1) * rows]


def gate(query, conv_t, pieces=2, width=1024):
    tok_rows, channels = query.shape
    width = min(width, channels)
    rows = tok_rows // pieces
    return pl.pallas_call(
        gate_kernel,
        grid=(channels // width,),
        out_shape=[jax.ShapeDtypeStruct((rows, channels), jnp.bfloat16)] * pieces,
        in_specs=[
            pl.BlockSpec((tok_rows, width), lambda i: (0, i)),
            pl.BlockSpec((width, tok_rows), lambda i: (i, 0)),
        ],
        out_specs=[pl.BlockSpec((rows, width), lambda i: (0, i))] * pieces,
        compiler_params=params(GRANT),
        cost_estimate=pl.CostEstimate(flops=tok_rows * channels, bytes_accessed=2 * MIB, transcendentals=0),
    )(query, conv_t)


def shift(array, axis, by):
    length = lax.axis_size(axis)
    return lax.ppermute(array, axis, [(i, (i + by) % length) for i in range(length)])


def project_kernel(*refs, count, pieces, has_total):
    blocks, weights = refs[: count * pieces], refs[count * pieces : count * (pieces + 1)]
    out_ref = refs[-1]
    total = refs[count * (pieces + 1)][...] if has_total else None
    for i in range(count):
        block = jnp.concatenate([ref[...] for ref in blocks[i * pieces : (i + 1) * pieces]], 0)
        term = jnp.dot(block, weights[i][...], preferred_element_type=jnp.float32)
        total = term if total is None else total + term
    out_ref[...] = total.astype(out_ref.dtype)


def project_part(blocks, weights, total, kind):
    count, pieces = len(blocks), len(blocks[0])
    rows, depth = blocks[0][0].shape
    columns = weights[0].shape[1]
    tok_rows = rows * pieces
    operands = [piece for block in blocks for piece in block] + weights + ([] if total is None else [total])
    return pl.pallas_call(
        functools.partial(project_kernel, count=count, pieces=pieces, has_total=total is not None),
        out_shape=jax.ShapeDtypeStruct((tok_rows, columns), kind),
        compiler_params=params(GRANT),
        cost_estimate=pl.CostEstimate(
            flops=2 * count * tok_rows * depth * columns,
            bytes_accessed=2 * count * depth * columns,
            transcendentals=0,
        ),
    )(*operands)


def project(pieces, w_out):
    size = lax.axis_size("ch")
    place = lax.axis_index("ch")
    depth = pieces[0].shape[1]
    own, after, far_rows, before = (
        lax.dynamic_slice_in_dim(w_out, (place + i) % size * depth, depth, 0) for i in range(size)
    )
    up, down = pieces
    right_up, left_down = shift(up, "ch", 1), shift(down, "ch", -1)
    right_down, left_up = shift(down, "ch", 1), shift(up, "ch", -1)
    far_up, far_down = shift(right_up, "ch", 1), shift(left_down, "ch", -1)
    total = project_part([(up, down)], [own], None, jnp.float32)
    near = [(right_up, right_down), (left_up, left_down)]
    total = project_part(near, [before, after], total, jnp.float32)
    return project_part([(far_up, far_down)], [far_rows], total, jnp.bfloat16)


def per_device(qkv, short_taps, lengths, filter_taps, w_out):
    tok_rows, _, width = qkv.shape
    lead = TAPS - 1
    seq = lax.axis_size("seq")
    by_kind = qkv.transpose(1, 0, 2)
    sent = products(lengths, by_kind, short_taps, seq)
    signal = lax.all_to_all(sent, "seq", 0, 0, tiled=True)
    conv = long_conv(lengths, signal, filter_taps[0], short_taps)
    late, conv = lax.optimization_barrier((by_kind, conv))
    edge = lax.ppermute(late[0, tok_rows - lead :], "seq", [(i, i + 1) for i in range(seq - 1)])
    query = queries(lengths, late, edge, short_taps)
    conv_t = lax.all_to_all(conv, "seq", 0, 0, tiled=True).reshape(width, tok_rows)
    return project(gate(query, conv_t), w_out)


def solution(mesh):
    placed = (P("seq", None, "ch"), P(None, None, "ch"), P(), P("ch", "seq", None), P(None, "ch"))
    return jax.shard_map(
        per_device, mesh=mesh, in_specs=placed, out_specs=P("seq", "ch"), check_vma=False
    )
```

```python
import functools

import jax
import jax.numpy as jnp
from jax import lax
from jax.experimental import pallas as pl
from jax.experimental.pallas import tpu as pltpu
from jax.sharding import PartitionSpec as P

TAPS = 3
BLK = 256
TILE = 128
PAD = 8
GRANT = 24
START_GRANT = 60
EDGES = 8
MIB = 1 << 20


def params(mib):
    return pltpu.CompilerParams(vmem_limit_bytes=mib * MIB)


def short_filter(scr, taps_ref, which, keeps_ref, lanes):
    tok_rows = scr.shape[0] - 8
    total = taps_ref[0, which : which + 1, lanes] * scr[8 : 8 + tok_rows, lanes]
    for tap in range(1, TAPS):
        window = scr[8 - tap : 8 - tap + tok_rows, lanes] * keeps_ref[tap - 1]
        total = total + taps_ref[tap, which : which + 1, lanes] * window
    return total


def fill(scr, values, edge=None):
    scr[:8, :] = jnp.zeros((8, scr.shape[1]), jnp.float32)
    if edge is not None:
        scr[6:8, :] = edge.astype(jnp.float32)
    scr[8:, :] = values.astype(jnp.float32)


def fill_keeps(lengths_ref, keeps_ref):
    @pl.when(pl.program_id(0) == 0)
    def _():
        _, tok_rows, width = keeps_ref.shape
        place = lax.axis_index("seq") * tok_rows
        positions = place + lax.broadcasted_iota(jnp.int32, (tok_rows, width), 0)
        starts = jnp.zeros((tok_rows, width), jnp.int32)
        offset = jnp.int32(0)
        for prompt in range(lengths_ref.shape[0]):
            starts = jnp.where(positions >= offset, offset, starts)
            offset = offset + lengths_ref[prompt]
        for tap in range(1, TAPS):
            keeps_ref[tap - 1] = (positions - tap >= starts).astype(jnp.float32)


def lane_parts(width):
    return [slice(i, i + TILE) for i in range(0, width, TILE)]


def product_kernel(lengths_ref, k_ref, v_ref, taps_ref, out_ref, keeps_ref, scr_k, scr_v):
    fill_keeps(lengths_ref, keeps_ref)
    fill(scr_k, k_ref[...])
    fill(scr_v, v_ref[...])
    tok_rows, width = k_ref.shape
    held = (out_ref.shape[1] - EDGES) * TILE // tok_rows
    for lanes in lane_parts(width):
        product = short_filter(scr_k, taps_ref, 1, keeps_ref, lanes) * short_filter(
            scr_v, taps_ref, 2, keeps_ref, lanes
        )
        product = product.T
        halves = [product[:, at : at + TILE] for at in range(0, tok_rows, TILE)]
        outer = [scr[8 + t : 10 + t, lanes] for scr in (scr_k, scr_v) for t in (0, tok_rows - 2)]
        outer = jnp.concatenate(outer, 0)
        for i in range(TILE // held):
            mine = outer if i == 0 else pltpu.roll(outer, TILE - i * held, 1)
            rows = jnp.concatenate([half[i * held : (i + 1) * held] for half in halves] + [mine], 0)
            out_ref[lanes.start // held + i] = rows.astype(jnp.bfloat16)


def query_kernel(lengths_ref, q_ref, edge_ref, taps_ref, out_ref, keeps_ref, scr_q):
    fill_keeps(lengths_ref, keeps_ref)
    fill(scr_q, q_ref[...], edge_ref[...])
    for lanes in lane_parts(q_ref.shape[1]):
        out_ref[:, lanes] = short_filter(scr_q, taps_ref, 0, keeps_ref, lanes).astype(jnp.bfloat16)


def short_call(kernel, lengths, by_kind, edge, taps, kinds, shape, block, grant, width=512):
    _, tok_rows, channels = by_kind.shape
    steps = channels // width
    return pl.pallas_call(
        kernel,
        grid=(steps,),
        out_shape=jax.ShapeDtypeStruct(shape, jnp.bfloat16),
        in_specs=[pl.BlockSpec(memory_space=pltpu.SMEM)]
        + [pl.BlockSpec((None, tok_rows, width), lambda i, kind=kind: (kind, 0, i)) for kind in kinds]
        + [pl.BlockSpec((TAPS - 1, width), lambda i: (0, i))] * (edge is not None)
        + [pl.BlockSpec((TAPS, 3, width), lambda i: (0, 0, i))],
        out_specs=block,
        scratch_shapes=[pltpu.VMEM((TAPS - 1, tok_rows, TILE), jnp.float32)]
        + [pltpu.VMEM((tok_rows + 8, width), jnp.float32)] * len(kinds),
        compiler_params=params(grant),
        cost_estimate=pl.CostEstimate(flops=20 * tok_rows * channels, bytes_accessed=2 * MIB, transcendentals=0),
    )(lengths, *([by_kind] * len(kinds)), *([] if edge is None else [edge]), taps)


def products(lengths, by_kind, taps, devices, width=512):
    _, tok_rows, channels = by_kind.shape
    held = channels // devices
    shape = (devices, held * tok_rows // TILE + EDGES, TILE)
    block = pl.BlockSpec((width // held,) + shape[1:], lambda i: (i, 0, 0))
    return short_call(product_kernel, lengths, by_kind, None, taps, (1, 2), shape, block, START_GRANT, width)


def queries(lengths, by_kind, edge, taps, width=512):
    _, tok_rows, channels = by_kind.shape
    block = pl.BlockSpec((tok_rows, width), lambda i: (0, i))
    return short_call(query_kernel, lengths, by_kind, edge, taps, (0,), (tok_rows, channels), block, GRANT, width)


def list_rows(lengths_ref, table, heads, rows):
    for row in range(rows - lengths_ref.shape[0], rows):
        for i in range(3):
            table[i, row] = jnp.int32(0)
    offset, row = jnp.int32(0), jnp.int32(0)
    for prompt in range(lengths_ref.shape[0]):
        end = offset + lengths_ref[prompt]
        first, last = offset // BLK, (end - 1) // BLK
        heads[1, prompt] = row

        def note(block, _, row=row, first=first, offset=offset, end=end):
            at = row + block - first
            table[0, at] = block
            table[1, at] = offset
            table[2, at] = end

            @pl.when(block * BLK >= offset)
            def _():
                heads[0, block] = at

            return 0

        lax.fori_loop(first, last + 1, note, 0)
        row = row + last - first + 1
        offset = end


def rows_before(lengths_ref, rows):
    row_ids = lax.broadcasted_iota(jnp.int32, (rows, TILE), 0)
    firsts = jnp.zeros((rows, TILE), jnp.int32)
    offset, row = jnp.int32(0), jnp.int32(0)
    for prompt in range(lengths_ref.shape[0]):
        firsts = jnp.where(row_ids >= row, row, firsts)
        end = offset + lengths_ref[prompt]
        row = row + (end - 1) // BLK - offset // BLK + 1
        offset = end
    return row_ids - firsts


def only_lanes(table, row, values, others):
    block, start, end = (table[i, row] for i in range(3))
    positions = block * BLK + lax.broadcasted_iota(jnp.int32, (8, BLK), 1)
    inside = (positions >= start) & (positions < end)
    shape = (values.shape[0] // 8, 8, BLK)
    others = others if isinstance(others, float) else others.reshape(shape)
    return jnp.where(inside[None], values.reshape(shape), others).reshape(values.shape)


def first_products(lengths_ref, edges, short_ref, channels):
    count = edges.shape[0]
    place = lax.axis_index("seq") * channels
    here = pl.ds(pl.multiple_of(place // TILE * TILE, TILE), TILE)
    rows = [short_ref[tap, which : which + 1, here] for which in (1, 2) for tap in range(TAPS)]
    rows = jnp.concatenate(rows + [jnp.zeros((2, TILE), jnp.float32)], 0)
    rows = pltpu.roll(rows, TILE - place % TILE, 1)
    columns = jnp.concatenate([rows, jnp.zeros((TILE - 8, TILE), jnp.float32)], 0).T[:channels]
    own = edges.T[:channels]
    lane = lax.broadcasted_iota(jnp.int32, (channels, count), 1)
    positions = lane // EDGES * BLK + lane % EDGES
    starts = jnp.zeros((channels, count), jnp.int32)
    offset = jnp.int32(0)
    for prompt in range(lengths_ref.shape[0]):
        starts = jnp.where(positions >= offset, offset, starts)
        offset = offset + lengths_ref[prompt]
    product = None
    for i in range(2):
        now = own if i == 0 else pltpu.roll(own, count - 4, 1)
        one = jnp.where(lane % EDGES == 0, pltpu.roll(now, 5, 1), pltpu.roll(now, 1, 1))
        two = pltpu.roll(now, 6, 1)
        total = columns[:, 3 * i : 3 * i + 1] * now
        for tap, value in ((1, one), (2, two)):
            keep = (positions - tap >= starts).astype(jnp.float32)
            total = total + columns[:, 3 * i + tap : 3 * i + tap + 1] * (value * keep)
        product = total if product is None else product * total
    return product.astype(jnp.bfloat16).astype(jnp.float32)


def pitch_of(rows):
    return rows | 1


def conv_kernel(
    lengths_ref, signal_ref, taps_ref, short_ref, out_ref, table, heads, blocks, edges, spread, result, before, toep, *, rows, rows_b
):
    devices, channels, _ = out_ref.shape
    span = taps_ref.shape[1]
    lags = span // BLK + 1
    tiles = span // TILE + 1
    pitch, held = pitch_of(PAD + rows_b), pitch_of(rows)

    list_rows(lengths_ref, table, heads, rows)
    for device in range(devices):
        arrived = signal_ref[device].astype(jnp.float32)
        for h in range(2):
            blocks[device, :, h * TILE : (h + 1) * TILE] = arrived[h * channels : (h + 1) * channels]
        edges[device * EDGES : (device + 1) * EDGES, :] = arrived[2 * channels :]
    firsts = first_products(lengths_ref, edges[...], short_ref, channels)
    is_first = lax.broadcasted_iota(jnp.int32, (channels, TILE), 1) < TAPS - 1
    for device in range(devices):
        at = device * EDGES
        mine = firsts[:, at // TILE * TILE : (at // TILE + 1) * TILE]
        mine = mine if at % TILE == 0 else pltpu.roll(mine, TILE - at % TILE, 1)
        blocks[device, :, :TILE] = jnp.where(is_first, mine, blocks[device, :, :TILE])
    for row in range(rows):
        slab = only_lanes(table, row, blocks[table[0, row]], 0.0)
        for h in range(2):
            spread[h, pl.ds(PAD + row, channels, stride=pitch), :] = slab[:, h * TILE : (h + 1) * TILE]
    before[...] = rows_before(lengths_ref, rows_b)

    zero = jnp.zeros((TILE, TILE), jnp.bfloat16)
    behind = before[...]

    def tile(g, t):
        return toep[g, t * TILE : (t + 1) * TILE, :] if 0 <= t < tiles else zero

    for g in range(channels):
        base = g * pitch + PAD
        row = jnp.concatenate([taps_ref[g : g + 1, :], jnp.zeros((1, TILE), jnp.float32)], 1)
        sheared = pltpu.roll(jnp.broadcast_to(row, (TILE, span + TILE)), 0, 1, stride=1, stride_axis=0)
        for t in range(tiles):
            toep[g, t * TILE : (t + 1) * TILE, :] = sheared[:, t * TILE : (t + 1) * TILE].astype(jnp.bfloat16)
        total = None
        for lag in range(lags):
            kept = behind >= lag
            left = jnp.concatenate(
                [
                    jnp.where(kept, spread[h, base - lag : base - lag + rows_b, :], 0.0).astype(jnp.bfloat16)
                    for h in range(2)
                ],
                1,
            )
            t = 2 * lag
            right = jnp.concatenate(
                [
                    jnp.concatenate([tile(g, t), tile(g, t + 1)], 1),
                    jnp.concatenate([tile(g, t - 1), tile(g, t)], 1),
                ],
                0,
            )
            term = jnp.dot(left, right, preferred_element_type=jnp.float32)
            total = term if total is None else total + term
        for h in range(2):
            result[h, g * held : g * held + rows, :] = total[:rows, h * TILE : (h + 1) * TILE]

    def slab_of(row):
        return jnp.concatenate([result[h, pl.ds(row, channels, stride=held), :] for h in range(2)], 1)

    for block in range(devices):
        out_ref[block] = slab_of(heads[0, block]).astype(jnp.bfloat16)
    for prompt in range(lengths_ref.shape[0]):
        row = heads[1, prompt]
        block = table[0, row]
        old = out_ref[block].astype(jnp.float32)
        out_ref[block] = only_lanes(table, row, slab_of(row), old).astype(jnp.bfloat16)


def round_up(value, to):
    return -(-value // to) * to


def long_conv(lengths, signal, taps, short_taps):
    devices, tok_rows = signal.shape[0], BLK
    channels = taps.shape[0]
    shape = (devices, channels, tok_rows)
    span = taps.shape[1]
    rows = round_up(devices + lengths.shape[0] - 1, 8)
    rows_b = round_up(rows, 16)
    return pl.pallas_call(
        functools.partial(conv_kernel, rows=rows, rows_b=rows_b),
        grid=(1,),
        out_shape=jax.ShapeDtypeStruct(shape, jnp.bfloat16),
        in_specs=[
            pl.BlockSpec(memory_space=pltpu.SMEM),
            pl.BlockSpec(signal.shape, lambda i: (0, 0, 0)),
            pl.BlockSpec((channels, span), lambda i: (0, 0)),
            pl.BlockSpec(short_taps.shape, lambda i: (0, 0, 0)),
        ],
        out_specs=pl.BlockSpec(shape, lambda i: (0, 0, 0)),
        scratch_shapes=[
            pltpu.SMEM((3, rows), jnp.int32),
            pltpu.SMEM((2, devices), jnp.int32),
            pltpu.VMEM(shape, jnp.float32),
            pltpu.VMEM((devices * EDGES, TILE), jnp.float32),
            pltpu.VMEM((2, round_up(channels * pitch_of(PAD + rows_b), 8), TILE), jnp.float32),
            pltpu.VMEM((2, round_up(channels * pitch_of(rows), 8), TILE), jnp.float32),
            pltpu.VMEM((rows_b, TILE), jnp.int32),
            pltpu.VMEM((channels, span + TILE, TILE), jnp.bfloat16),
        ],
        compiler_params=params(GRANT),
        cost_estimate=pl.CostEstimate(
            flops=2 * channels * rows * (span + BLK) * BLK, bytes_accessed=2 * MIB, transcendentals=0
        ),
    )(lengths, signal, taps, short_taps)


def gate_kernel(query_ref, conv_ref, *out_refs):
    conv = conv_ref[...].astype(jnp.float32).T
    gated = (query_ref[...].astype(jnp.float32) * conv).astype(jnp.bfloat16)
    rows = gated.shape[0] // len(out_refs)
    for i, out_ref in enumerate(out_refs):
        out_ref[...] = gated[i * rows : (i + 1) * rows]


def gate(query, conv_t, pieces=2, width=1024):
    tok_rows, channels = query.shape
    width = min(width, channels)
    rows = tok_rows // pieces
    return pl.pallas_call(
        gate_kernel,
        grid=(channels // width,),
        out_shape=[jax.ShapeDtypeStruct((rows, channels), jnp.bfloat16)] * pieces,
        in_specs=[
            pl.BlockSpec((tok_rows, width), lambda i: (0, i)),
            pl.BlockSpec((width, tok_rows), lambda i: (i, 0)),
        ],
        out_specs=[pl.BlockSpec((rows, width), lambda i: (0, i))] * pieces,
        compiler_params=params(GRANT),
        cost_estimate=pl.CostEstimate(flops=tok_rows * channels, bytes_accessed=2 * MIB, transcendentals=0),
    )(query, conv_t)


def shift(array, axis, by):
    length = lax.axis_size(axis)
    return lax.ppermute(array, axis, [(i, (i + by) % length) for i in range(length)])


def project_kernel(*refs, count, pieces, has_total):
    blocks, weights = refs[: count * pieces], refs[count * pieces : count * (pieces + 1)]
    out_ref = refs[-1]
    total = refs[count * (pieces + 1)][...] if has_total else None
    for i in range(count):
        block = jnp.concatenate([ref[...] for ref in blocks[i * pieces : (i + 1) * pieces]], 0)
        term = jnp.dot(block, weights[i][...], preferred_element_type=jnp.float32)
        total = term if total is None else total + term
    out_ref[...] = total.astype(out_ref.dtype)


def project_part(blocks, weights, total, kind):
    count, pieces = len(blocks), len(blocks[0])
    rows, depth = blocks[0][0].shape
    columns = weights[0].shape[1]
    tok_rows = rows * pieces
    operands = [piece for block in blocks for piece in block] + weights + ([] if total is None else [total])
    return pl.pallas_call(
        functools.partial(project_kernel, count=count, pieces=pieces, has_total=total is not None),
        out_shape=jax.ShapeDtypeStruct((tok_rows, columns), kind),
        compiler_params=params(GRANT),
        cost_estimate=pl.CostEstimate(
            flops=2 * count * tok_rows * depth * columns,
            bytes_accessed=2 * count * depth * columns,
            transcendentals=0,
        ),
    )(*operands)


def project(pieces, w_out):
    size = lax.axis_size("ch")
    place = lax.axis_index("ch")
    depth = pieces[0].shape[1]
    own, after, far_rows, before = (
        lax.dynamic_slice_in_dim(w_out, (place + i) % size * depth, depth, 0) for i in range(size)
    )
    up, down = pieces
    right_up, left_down = shift(up, "ch", 1), shift(down, "ch", -1)
    right_down, left_up = shift(down, "ch", 1), shift(up, "ch", -1)
    far_up, far_down = shift(right_up, "ch", 1), shift(left_down, "ch", -1)
    total = project_part([(up, down)], [own], None, jnp.float32)
    near = [(right_up, right_down), (left_up, left_down)]
    total = project_part(near, [before, after], total, jnp.float32)
    return project_part([(far_up, far_down)], [far_rows], total, jnp.bfloat16)


def per_device(qkv, short_taps, lengths, filter_taps, w_out):
    tok_rows, _, width = qkv.shape
    lead = TAPS - 1
    seq = lax.axis_size("seq")
    by_kind = qkv.transpose(1, 0, 2)
    sent = products(lengths, by_kind, short_taps, seq)
    signal = lax.all_to_all(sent, "seq", 0, 0, tiled=True)
    conv = long_conv(lengths, signal, filter_taps[0], short_taps)
    late, conv = lax.optimization_barrier((by_kind, conv))
    edge = lax.ppermute(late[0, tok_rows - lead :], "seq", [(i, i + 1) for i in range(seq - 1)])
    query = queries(lengths, late, edge, short_taps)
    conv_t = lax.all_to_all(conv, "seq", 0, 0, tiled=True).reshape(width, tok_rows)
    return project(gate(query, conv_t), w_out)


def solution(mesh):
    placed = (P("seq", None, "ch"), P(None, None, "ch"), P(), P("ch", "seq", None), P(None, "ch"))
    return jax.shard_map(
        per_device, mesh=mesh, in_specs=placed, out_specs=P("seq", "ch"), check_vma=False
    )
```

```python
import functools

import jax
import jax.numpy as jnp
from jax import lax
from jax.experimental import pallas as pl
from jax.experimental.pallas import tpu as pltpu
from jax.sharding import PartitionSpec as P

TAPS = 3
BLK = 256
TILE = 128
PAD = 8
GRANT = 24
START_GRANT = 60
EDGES = 8
MIB = 1 << 20


def params(mib):
    return pltpu.CompilerParams(vmem_limit_bytes=mib * MIB)


def short_filter(scr, taps_ref, which, keeps_ref, lanes):
    tok_rows = scr.shape[0] - 8
    total = taps_ref[0, which : which + 1, lanes] * scr[8 : 8 + tok_rows, lanes]
    for tap in range(1, TAPS):
        window = scr[8 - tap : 8 - tap + tok_rows, lanes] * keeps_ref[tap - 1]
        total = total + taps_ref[tap, which : which + 1, lanes] * window
    return total


def fill(scr, values, edge=None):
    scr[:8, :] = jnp.zeros((8, scr.shape[1]), jnp.float32)
    if edge is not None:
        scr[6:8, :] = edge.astype(jnp.float32)
    scr[8:, :] = values.astype(jnp.float32)


def fill_keeps(lengths_ref, keeps_ref):
    @pl.when(pl.program_id(0) == 0)
    def _():
        _, tok_rows, width = keeps_ref.shape
        place = lax.axis_index("seq") * tok_rows
        positions = place + lax.broadcasted_iota(jnp.int32, (tok_rows, width), 0)
        starts = jnp.zeros((tok_rows, width), jnp.int32)
        offset = jnp.int32(0)
        for prompt in range(lengths_ref.shape[0]):
            starts = jnp.where(positions >= offset, offset, starts)
            offset = offset + lengths_ref[prompt]
        for tap in range(1, TAPS):
            keeps_ref[tap - 1] = (positions - tap >= starts).astype(jnp.float32)


def lane_parts(width):
    return [slice(i, i + TILE) for i in range(0, width, TILE)]


def product_kernel(lengths_ref, k_ref, v_ref, taps_ref, out_ref, keeps_ref, scr_k, scr_v):
    fill_keeps(lengths_ref, keeps_ref)
    fill(scr_k, k_ref[...])
    fill(scr_v, v_ref[...])
    tok_rows, width = k_ref.shape
    held = (out_ref.shape[1] - EDGES) * TILE // tok_rows
    for lanes in lane_parts(width):
        product = short_filter(scr_k, taps_ref, 1, keeps_ref, lanes) * short_filter(
            scr_v, taps_ref, 2, keeps_ref, lanes
        )
        product = product.T
        halves = [product[:, at : at + TILE] for at in range(0, tok_rows, TILE)]
        outer = [scr[8 + t : 10 + t, lanes] for scr in (scr_k, scr_v) for t in (0, tok_rows - 2)]
        outer = jnp.concatenate(outer, 0)
        for i in range(TILE // held):
            mine = outer if i == 0 else pltpu.roll(outer, TILE - i * held, 1)
            rows = jnp.concatenate([half[i * held : (i + 1) * held] for half in halves] + [mine], 0)
            out_ref[lanes.start // held + i] = rows.astype(jnp.bfloat16)


def query_kernel(lengths_ref, q_ref, edge_ref, taps_ref, out_ref, keeps_ref, scr_q):
    fill_keeps(lengths_ref, keeps_ref)
    fill(scr_q, q_ref[...], edge_ref[...])
    for lanes in lane_parts(q_ref.shape[1]):
        out_ref[:, lanes] = short_filter(scr_q, taps_ref, 0, keeps_ref, lanes).astype(jnp.bfloat16)


def short_call(kernel, lengths, by_kind, edge, taps, kinds, shape, block, grant, width=512):
    _, tok_rows, channels = by_kind.shape
    steps = channels // width
    return pl.pallas_call(
        kernel,
        grid=(steps,),
        out_shape=jax.ShapeDtypeStruct(shape, jnp.bfloat16),
        in_specs=[pl.BlockSpec(memory_space=pltpu.SMEM)]
        + [pl.BlockSpec((None, tok_rows, width), lambda i, kind=kind: (kind, 0, i)) for kind in kinds]
        + [pl.BlockSpec((TAPS - 1, width), lambda i: (0, i))] * (edge is not None)
        + [pl.BlockSpec((TAPS, 3, width), lambda i: (0, 0, i))],
        out_specs=block,
        scratch_shapes=[pltpu.VMEM((TAPS - 1, tok_rows, TILE), jnp.float32)]
        + [pltpu.VMEM((tok_rows + 8, width), jnp.float32)] * len(kinds),
        compiler_params=params(grant),
        cost_estimate=pl.CostEstimate(flops=20 * tok_rows * channels, bytes_accessed=2 * MIB, transcendentals=0),
    )(lengths, *([by_kind] * len(kinds)), *([] if edge is None else [edge]), taps)


def products(lengths, by_kind, taps, devices, width=512):
    _, tok_rows, channels = by_kind.shape
    held = channels // devices
    shape = (devices, held * tok_rows // TILE + EDGES, TILE)
    block = pl.BlockSpec((width // held,) + shape[1:], lambda i: (i, 0, 0))
    return short_call(product_kernel, lengths, by_kind, None, taps, (1, 2), shape, block, START_GRANT, width)


def queries(lengths, by_kind, edge, taps, width=512):
    _, tok_rows, channels = by_kind.shape
    block = pl.BlockSpec((tok_rows, width), lambda i: (0, i))
    return short_call(query_kernel, lengths, by_kind, edge, taps, (0,), (tok_rows, channels), block, GRANT, width)


def list_rows(lengths_ref, table, heads, rows):
    for row in range(rows - lengths_ref.shape[0], rows):
        for i in range(3):
            table[i, row] = jnp.int32(0)
    offset, row = jnp.int32(0), jnp.int32(0)
    for prompt in range(lengths_ref.shape[0]):
        end = offset + lengths_ref[prompt]
        first, last = offset // BLK, (end - 1) // BLK
        heads[1, prompt] = row

        def note(block, _, row=row, first=first, offset=offset, end=end):
            at = row + block - first
            table[0, at] = block
            table[1, at] = offset
            table[2, at] = end

            @pl.when(block * BLK >= offset)
            def _():
                heads[0, block] = at

            return 0

        lax.fori_loop(first, last + 1, note, 0)
        row = row + last - first + 1
        offset = end


def rows_before(lengths_ref, rows):
    row_ids = lax.broadcasted_iota(jnp.int32, (rows, TILE), 0)
    firsts = jnp.zeros((rows, TILE), jnp.int32)
    offset, row = jnp.int32(0), jnp.int32(0)
    for prompt in range(lengths_ref.shape[0]):
        firsts = jnp.where(row_ids >= row, row, firsts)
        end = offset + lengths_ref[prompt]
        row = row + (end - 1) // BLK - offset // BLK + 1
        offset = end
    return row_ids - firsts


def only_lanes(table, row, values, others):
    block, start, end = (table[i, row] for i in range(3))
    positions = block * BLK + lax.broadcasted_iota(jnp.int32, (8, BLK), 1)
    inside = (positions >= start) & (positions < end)
    shape = (values.shape[0] // 8, 8, BLK)
    others = others if isinstance(others, float) else others.reshape(shape)
    return jnp.where(inside[None], values.reshape(shape), others).reshape(values.shape)


def first_products(lengths_ref, edges, short_ref, channels):
    count = edges.shape[0]
    place = lax.axis_index("seq") * channels
    here = pl.ds(pl.multiple_of(place // TILE * TILE, TILE), TILE)
    rows = [short_ref[tap, which : which + 1, here] for which in (1, 2) for tap in range(TAPS)]
    rows = jnp.concatenate(rows + [jnp.zeros((2, TILE), jnp.float32)], 0)
    rows = pltpu.roll(rows, TILE - place % TILE, 1)
    columns = jnp.concatenate([rows, jnp.zeros((TILE - 8, TILE), jnp.float32)], 0).T[:channels]
    own = edges.T[:channels]
    lane = lax.broadcasted_iota(jnp.int32, (channels, count), 1)
    positions = lane // EDGES * BLK + lane % EDGES
    starts = jnp.zeros((channels, count), jnp.int32)
    offset = jnp.int32(0)
    for prompt in range(lengths_ref.shape[0]):
        starts = jnp.where(positions >= offset, offset, starts)
        offset = offset + lengths_ref[prompt]
    product = None
    for i in range(2):
        now = own if i == 0 else pltpu.roll(own, count - 4, 1)
        one = jnp.where(lane % EDGES == 0, pltpu.roll(now, 5, 1), pltpu.roll(now, 1, 1))
        two = pltpu.roll(now, 6, 1)
        total = columns[:, 3 * i : 3 * i + 1] * now
        for tap, value in ((1, one), (2, two)):
            keep = (positions - tap >= starts).astype(jnp.float32)
            total = total + columns[:, 3 * i + tap : 3 * i + tap + 1] * (value * keep)
        product = total if product is None else product * total
    return product.astype(jnp.bfloat16).astype(jnp.float32)


def pitch_of(rows):
    return rows | 1


def conv_kernel(
    lengths_ref, signal_ref, taps_ref, short_ref, out_ref, table, heads, blocks, edges, spread, result, before, toep, *, rows, rows_b
):
    devices, channels, _ = out_ref.shape
    span = taps_ref.shape[1]
    lags = span // BLK + 1
    tiles = span // TILE + 1
    pitch, held = pitch_of(PAD + rows_b), pitch_of(rows)

    list_rows(lengths_ref, table, heads, rows)
    for device in range(devices):
        arrived = signal_ref[device].astype(jnp.float32)
        for h in range(2):
            blocks[device, :, h * TILE : (h + 1) * TILE] = arrived[h * channels : (h + 1) * channels]
        edges[device * EDGES : (device + 1) * EDGES, :] = arrived[2 * channels :]
    firsts = first_products(lengths_ref, edges[...], short_ref, channels)
    is_first = lax.broadcasted_iota(jnp.int32, (channels, TILE), 1) < TAPS - 1
    for device in range(devices):
        at = device * EDGES
        mine = firsts[:, at // TILE * TILE : (at // TILE + 1) * TILE]
        mine = mine if at % TILE == 0 else pltpu.roll(mine, TILE - at % TILE, 1)
        blocks[device, :, :TILE] = jnp.where(is_first, mine, blocks[device, :, :TILE])
    for row in range(rows):
        slab = only_lanes(table, row, blocks[table[0, row]], 0.0)
        for h in range(2):
            spread[h, pl.ds(PAD + row, channels, stride=pitch), :] = slab[:, h * TILE : (h + 1) * TILE]
    before[...] = rows_before(lengths_ref, rows_b)

    behind = before[...]

    def tile(g, t):
        return toep[g, t * TILE : (t + 1) * TILE, :]

    for g in range(channels):
        base = g * pitch + PAD
        row = jnp.concatenate([taps_ref[g : g + 1, :], jnp.zeros((1, TILE), jnp.float32)], 1)
        sheared = pltpu.roll(jnp.broadcast_to(row, (TILE, span + TILE)), 0, 1, stride=1, stride_axis=0)
        for t in range(tiles):
            toep[g, t * TILE : (t + 1) * TILE, :] = sheared[:, t * TILE : (t + 1) * TILE].astype(jnp.bfloat16)
        lefts = [
            [
                jnp.where(behind >= lag, spread[h, base - lag : base - lag + rows_b, :], 0.0).astype(jnp.bfloat16)
                for h in range(2)
            ]
            for lag in range(lags)
        ]
        last = lags - 1
        both = jnp.concatenate([lefts[last][0], lefts[0][1]], 0)
        both = jnp.dot(both, jnp.concatenate([tile(g, 2 * last), tile(g, 0)], 1), preferred_element_type=jnp.float32)
        total = jnp.concatenate([both[:rows_b, :TILE], both[rows_b:, TILE:]], 1)
        for lag in range(last):
            t = 2 * lag
            if lag == 0:
                left = [lefts[0][0], lefts[last][1]]
                lower = [tile(g, 2 * last - 1), tile(g, 2 * last)]
            else:
                left = lefts[lag]
                lower = [tile(g, t - 1), tile(g, t)]
            right = [jnp.concatenate([tile(g, t), tile(g, t + 1)], 1), jnp.concatenate(lower, 1)]
            total = total + jnp.dot(
                jnp.concatenate(left, 1), jnp.concatenate(right, 0), preferred_element_type=jnp.float32
            )
        for h in range(2):
            result[h, g * held : g * held + rows, :] = total[:rows, h * TILE : (h + 1) * TILE]

    def slab_of(row):
        return jnp.concatenate([result[h, pl.ds(row, channels, stride=held), :] for h in range(2)], 1)

    for block in range(devices):
        out_ref[block] = slab_of(heads[0, block]).astype(jnp.bfloat16)
    for prompt in range(lengths_ref.shape[0]):
        row = heads[1, prompt]
        block = table[0, row]
        old = out_ref[block].astype(jnp.float32)
        out_ref[block] = only_lanes(table, row, slab_of(row), old).astype(jnp.bfloat16)


def round_up(value, to):
    return -(-value // to) * to


def long_conv(lengths, signal, taps, short_taps):
    devices, tok_rows = signal.shape[0], BLK
    channels = taps.shape[0]
    shape = (devices, channels, tok_rows)
    span = taps.shape[1]
    rows = round_up(devices + lengths.shape[0] - 1, 8)
    rows_b = round_up(rows, 16)
    return pl.pallas_call(
        functools.partial(conv_kernel, rows=rows, rows_b=rows_b),
        grid=(1,),
        out_shape=jax.ShapeDtypeStruct(shape, jnp.bfloat16),
        in_specs=[
            pl.BlockSpec(memory_space=pltpu.SMEM),
            pl.BlockSpec(signal.shape, lambda i: (0, 0, 0)),
            pl.BlockSpec((channels, span), lambda i: (0, 0)),
            pl.BlockSpec(short_taps.shape, lambda i: (0, 0, 0)),
        ],
        out_specs=pl.BlockSpec(shape, lambda i: (0, 0, 0)),
        scratch_shapes=[
            pltpu.SMEM((3, rows), jnp.int32),
            pltpu.SMEM((2, devices), jnp.int32),
            pltpu.VMEM(shape, jnp.float32),
            pltpu.VMEM((devices * EDGES, TILE), jnp.float32),
            pltpu.VMEM((2, round_up(channels * pitch_of(PAD + rows_b), 8), TILE), jnp.float32),
            pltpu.VMEM((2, round_up(channels * pitch_of(rows), 8), TILE), jnp.float32),
            pltpu.VMEM((rows_b, TILE), jnp.int32),
            pltpu.VMEM((channels, span + TILE, TILE), jnp.bfloat16),
        ],
        compiler_params=params(GRANT),
        cost_estimate=pl.CostEstimate(
            flops=2 * channels * rows * (span + BLK) * BLK, bytes_accessed=2 * MIB, transcendentals=0
        ),
    )(lengths, signal, taps, short_taps)


def gate_kernel(query_ref, conv_ref, *out_refs):
    conv = conv_ref[...].astype(jnp.float32).T
    gated = (query_ref[...].astype(jnp.float32) * conv).astype(jnp.bfloat16)
    rows = gated.shape[0] // len(out_refs)
    for i, out_ref in enumerate(out_refs):
        out_ref[...] = gated[i * rows : (i + 1) * rows]


def gate(query, conv_t, pieces=2, width=1024):
    tok_rows, channels = query.shape
    width = min(width, channels)
    rows = tok_rows // pieces
    return pl.pallas_call(
        gate_kernel,
        grid=(channels // width,),
        out_shape=[jax.ShapeDtypeStruct((rows, channels), jnp.bfloat16)] * pieces,
        in_specs=[
            pl.BlockSpec((tok_rows, width), lambda i: (0, i)),
            pl.BlockSpec((width, tok_rows), lambda i: (i, 0)),
        ],
        out_specs=[pl.BlockSpec((rows, width), lambda i: (0, i))] * pieces,
        compiler_params=params(GRANT),
        cost_estimate=pl.CostEstimate(flops=tok_rows * channels, bytes_accessed=2 * MIB, transcendentals=0),
    )(query, conv_t)


def shift(array, axis, by):
    length = lax.axis_size(axis)
    return lax.ppermute(array, axis, [(i, (i + by) % length) for i in range(length)])


def project_kernel(*refs, count, pieces, has_total):
    blocks, weights = refs[: count * pieces], refs[count * pieces : count * (pieces + 1)]
    out_ref = refs[-1]
    total = refs[count * (pieces + 1)][...] if has_total else None
    for i in range(count):
        block = jnp.concatenate([ref[...] for ref in blocks[i * pieces : (i + 1) * pieces]], 0)
        term = jnp.dot(block, weights[i][...], preferred_element_type=jnp.float32)
        total = term if total is None else total + term
    out_ref[...] = total.astype(out_ref.dtype)


def project_part(blocks, weights, total, kind):
    count, pieces = len(blocks), len(blocks[0])
    rows, depth = blocks[0][0].shape
    columns = weights[0].shape[1]
    tok_rows = rows * pieces
    operands = [piece for block in blocks for piece in block] + weights + ([] if total is None else [total])
    return pl.pallas_call(
        functools.partial(project_kernel, count=count, pieces=pieces, has_total=total is not None),
        out_shape=jax.ShapeDtypeStruct((tok_rows, columns), kind),
        compiler_params=params(GRANT),
        cost_estimate=pl.CostEstimate(
            flops=2 * count * tok_rows * depth * columns,
            bytes_accessed=2 * count * depth * columns,
            transcendentals=0,
        ),
    )(*operands)


def project(pieces, w_out):
    size = lax.axis_size("ch")
    place = lax.axis_index("ch")
    depth = pieces[0].shape[1]
    own, after, far_rows, before = (
        lax.dynamic_slice_in_dim(w_out, (place + i) % size * depth, depth, 0) for i in range(size)
    )
    up, down = pieces
    right_up, left_down = shift(up, "ch", 1), shift(down, "ch", -1)
    right_down, left_up = shift(down, "ch", 1), shift(up, "ch", -1)
    far_up, far_down = shift(right_up, "ch", 1), shift(left_down, "ch", -1)
    total = project_part([(up, down)], [own], None, jnp.float32)
    near = [(right_up, right_down), (left_up, left_down)]
    total = project_part(near, [before, after], total, jnp.float32)
    return project_part([(far_up, far_down)], [far_rows], total, jnp.bfloat16)


def per_device(qkv, short_taps, lengths, filter_taps, w_out):
    tok_rows, _, width = qkv.shape
    lead = TAPS - 1
    seq = lax.axis_size("seq")
    by_kind = qkv.transpose(1, 0, 2)
    sent = products(lengths, by_kind, short_taps, seq)
    signal = lax.all_to_all(sent, "seq", 0, 0, tiled=True)
    conv = long_conv(lengths, signal, filter_taps[0], short_taps)
    late, conv = lax.optimization_barrier((by_kind, conv))
    edge = lax.ppermute(late[0, tok_rows - lead :], "seq", [(i, i + 1) for i in range(seq - 1)])
    query = queries(lengths, late, edge, short_taps)
    conv_t = lax.all_to_all(conv, "seq", 0, 0, tiled=True).reshape(width, tok_rows)
    return project(gate(query, conv_t), w_out)


def solution(mesh):
    placed = (P("seq", None, "ch"), P(None, None, "ch"), P(), P("ch", "seq", None), P(None, "ch"))
    return jax.shard_map(
        per_device, mesh=mesh, in_specs=placed, out_specs=P("seq", "ch"), check_vma=False
    )
```

```python
import functools

import jax
import jax.numpy as jnp
from jax import lax
from jax.experimental import pallas as pl
from jax.experimental.pallas import tpu as pltpu
from jax.sharding import PartitionSpec as P

TAPS = 3
BLK = 256
TILE = 128
PAD = 8
GRANT = 24
START_GRANT = 60
EDGES = 8
MIB = 1 << 20


def params(mib):
    return pltpu.CompilerParams(vmem_limit_bytes=mib * MIB)


def short_filter(scr, taps_ref, which, keeps_ref, lanes):
    tok_rows = scr.shape[0] - 8
    total = taps_ref[0, which : which + 1, lanes] * scr[8 : 8 + tok_rows, lanes]
    for tap in range(1, TAPS):
        window = scr[8 - tap : 8 - tap + tok_rows, lanes] * keeps_ref[tap - 1]
        total = total + taps_ref[tap, which : which + 1, lanes] * window
    return total


def fill(scr, values, edge=None):
    scr[:8, :] = jnp.zeros((8, scr.shape[1]), jnp.float32)
    if edge is not None:
        scr[6:8, :] = edge.astype(jnp.float32)
    scr[8:, :] = values.astype(jnp.float32)


def fill_keeps(lengths_ref, keeps_ref):
    @pl.when(pl.program_id(0) == 0)
    def _():
        _, tok_rows, width = keeps_ref.shape
        place = lax.axis_index("seq") * tok_rows
        positions = place + lax.broadcasted_iota(jnp.int32, (tok_rows, width), 0)
        starts = jnp.zeros((tok_rows, width), jnp.int32)
        offset = jnp.int32(0)
        for prompt in range(lengths_ref.shape[0]):
            starts = jnp.where(positions >= offset, offset, starts)
            offset = offset + lengths_ref[prompt]
        for tap in range(1, TAPS):
            keeps_ref[tap - 1] = (positions - tap >= starts).astype(jnp.float32)


def lane_parts(width):
    return [slice(i, i + TILE) for i in range(0, width, TILE)]


def product_kernel(lengths_ref, k_ref, v_ref, taps_ref, out_ref, keeps_ref, scr_k, scr_v):
    fill_keeps(lengths_ref, keeps_ref)
    fill(scr_k, k_ref[...])
    fill(scr_v, v_ref[...])
    tok_rows, width = k_ref.shape
    held = (out_ref.shape[1] - EDGES) * TILE // tok_rows
    for lanes in lane_parts(width):
        product = short_filter(scr_k, taps_ref, 1, keeps_ref, lanes) * short_filter(
            scr_v, taps_ref, 2, keeps_ref, lanes
        )
        product = product.T
        halves = [product[:, at : at + TILE] for at in range(0, tok_rows, TILE)]
        outer = [scr[8 + t : 10 + t, lanes] for scr in (scr_k, scr_v) for t in (0, tok_rows - 2)]
        outer = jnp.concatenate(outer, 0)
        for i in range(TILE // held):
            mine = outer if i == 0 else pltpu.roll(outer, TILE - i * held, 1)
            rows = jnp.concatenate([half[i * held : (i + 1) * held] for half in halves] + [mine], 0)
            out_ref[lanes.start // held + i] = rows.astype(jnp.bfloat16)


def query_kernel(lengths_ref, q_ref, edge_ref, taps_ref, out_ref, keeps_ref, scr_q):
    fill_keeps(lengths_ref, keeps_ref)
    fill(scr_q, q_ref[...], edge_ref[...])
    for lanes in lane_parts(q_ref.shape[1]):
        out_ref[:, lanes] = short_filter(scr_q, taps_ref, 0, keeps_ref, lanes).astype(jnp.bfloat16)


def short_call(kernel, lengths, by_kind, edge, taps, kinds, shape, block, grant, width=512):
    _, tok_rows, channels = by_kind.shape
    steps = channels // width
    return pl.pallas_call(
        kernel,
        grid=(steps,),
        out_shape=jax.ShapeDtypeStruct(shape, jnp.bfloat16),
        in_specs=[pl.BlockSpec(memory_space=pltpu.SMEM)]
        + [pl.BlockSpec((None, tok_rows, width), lambda i, kind=kind: (kind, 0, i)) for kind in kinds]
        + [pl.BlockSpec((TAPS - 1, width), lambda i: (0, i))] * (edge is not None)
        + [pl.BlockSpec((TAPS, 3, width), lambda i: (0, 0, i))],
        out_specs=block,
        scratch_shapes=[pltpu.VMEM((TAPS - 1, tok_rows, TILE), jnp.float32)]
        + [pltpu.VMEM((tok_rows + 8, width), jnp.float32)] * len(kinds),
        compiler_params=params(grant),
        cost_estimate=pl.CostEstimate(flops=20 * tok_rows * channels, bytes_accessed=2 * MIB, transcendentals=0),
    )(lengths, *([by_kind] * len(kinds)), *([] if edge is None else [edge]), taps)


def products(lengths, by_kind, taps, devices, width=512):
    _, tok_rows, channels = by_kind.shape
    held = channels // devices
    shape = (devices, held * tok_rows // TILE + EDGES, TILE)
    block = pl.BlockSpec((width // held,) + shape[1:], lambda i: (i, 0, 0))
    return short_call(product_kernel, lengths, by_kind, None, taps, (1, 2), shape, block, START_GRANT, width)


def queries(lengths, by_kind, edge, taps, width=512):
    _, tok_rows, channels = by_kind.shape
    block = pl.BlockSpec((tok_rows, width), lambda i: (0, i))
    return short_call(query_kernel, lengths, by_kind, edge, taps, (0,), (tok_rows, channels), block, GRANT, width)


def list_rows(lengths_ref, table, heads, rows):
    for row in range(rows - lengths_ref.shape[0], rows):
        for i in range(3):
            table[i, row] = jnp.int32(0)
    offset, row = jnp.int32(0), jnp.int32(0)
    for prompt in range(lengths_ref.shape[0]):
        end = offset + lengths_ref[prompt]
        first, last = offset // BLK, (end - 1) // BLK
        heads[1, prompt] = row

        def note(block, _, row=row, first=first, offset=offset, end=end):
            at = row + block - first
            table[0, at] = block
            table[1, at] = offset
            table[2, at] = end

            @pl.when(block * BLK >= offset)
            def _():
                heads[0, block] = at

            return 0

        lax.fori_loop(first, last + 1, note, 0)
        row = row + last - first + 1
        offset = end


def rows_before(lengths_ref, rows):
    row_ids = lax.broadcasted_iota(jnp.int32, (rows, TILE), 0)
    firsts = jnp.zeros((rows, TILE), jnp.int32)
    offset, row = jnp.int32(0), jnp.int32(0)
    for prompt in range(lengths_ref.shape[0]):
        firsts = jnp.where(row_ids >= row, row, firsts)
        end = offset + lengths_ref[prompt]
        row = row + (end - 1) // BLK - offset // BLK + 1
        offset = end
    return row_ids - firsts


def only_lanes(table, row, values, others):
    block, start, end = (table[i, row] for i in range(3))
    positions = block * BLK + lax.broadcasted_iota(jnp.int32, (8, BLK), 1)
    inside = (positions >= start) & (positions < end)
    shape = (values.shape[0] // 8, 8, BLK)
    others = others if isinstance(others, float) else others.reshape(shape)
    return jnp.where(inside[None], values.reshape(shape), others).reshape(values.shape)


def first_products(lengths_ref, edges, short_ref, channels):
    count = edges.shape[0]
    place = lax.axis_index("seq") * channels
    here = pl.ds(pl.multiple_of(place // TILE * TILE, TILE), TILE)
    rows = [short_ref[tap, which : which + 1, here] for which in (1, 2) for tap in range(TAPS)]
    rows = jnp.concatenate(rows + [jnp.zeros((2, TILE), jnp.float32)], 0)
    rows = pltpu.roll(rows, TILE - place % TILE, 1)
    columns = jnp.concatenate([rows, jnp.zeros((TILE - 8, TILE), jnp.float32)], 0).T[:channels]
    own = edges.T[:channels]
    lane = lax.broadcasted_iota(jnp.int32, (channels, count), 1)
    positions = lane // EDGES * BLK + lane % EDGES
    starts = jnp.zeros((channels, count), jnp.int32)
    offset = jnp.int32(0)
    for prompt in range(lengths_ref.shape[0]):
        starts = jnp.where(positions >= offset, offset, starts)
        offset = offset + lengths_ref[prompt]
    product = None
    for i in range(2):
        now = own if i == 0 else pltpu.roll(own, count - 4, 1)
        one = jnp.where(lane % EDGES == 0, pltpu.roll(now, 5, 1), pltpu.roll(now, 1, 1))
        two = pltpu.roll(now, 6, 1)
        total = columns[:, 3 * i : 3 * i + 1] * now
        for tap, value in ((1, one), (2, two)):
            keep = (positions - tap >= starts).astype(jnp.float32)
            total = total + columns[:, 3 * i + tap : 3 * i + tap + 1] * (value * keep)
        product = total if product is None else product * total
    return product.astype(jnp.bfloat16).astype(jnp.float32)


def pitch_of(rows):
    return rows | 1


def conv_kernel(
    lengths_ref, signal_ref, taps_ref, short_ref, out_ref, table, heads, blocks, edges, spread, result, before, toep, *, rows, rows_b
):
    devices, channels, _ = out_ref.shape
    span = taps_ref.shape[1]
    lags = span // BLK + 1
    tiles = span // TILE + 1
    pitch, held = pitch_of(PAD + rows_b), pitch_of(rows)

    list_rows(lengths_ref, table, heads, rows)
    for device in range(devices):
        edges[device * EDGES : (device + 1) * EDGES, :] = signal_ref[device].astype(jnp.float32)[2 * channels :]
    firsts = first_products(lengths_ref, edges[...], short_ref, channels)
    is_first = lax.broadcasted_iota(jnp.int32, (channels, TILE), 1) < TAPS - 1
    for device in range(devices):
        arrived = signal_ref[device].astype(jnp.float32)
        at = device * EDGES
        mine = firsts[:, at // TILE * TILE : (at // TILE + 1) * TILE]
        mine = mine if at % TILE == 0 else pltpu.roll(mine, TILE - at % TILE, 1)
        blocks[device, :, :TILE] = jnp.where(is_first, mine, arrived[:channels])
        blocks[device, :, TILE:] = arrived[channels : 2 * channels]
    for row in range(rows):
        slab = only_lanes(table, row, blocks[table[0, row]], 0.0)
        for h in range(2):
            spread[h, pl.ds(PAD + row, channels, stride=pitch), :] = slab[:, h * TILE : (h + 1) * TILE]
    before[...] = rows_before(lengths_ref, rows_b)

    behind = before[...]

    def tile(g, t):
        return toep[g, t * TILE : (t + 1) * TILE, :]

    for g in range(channels):
        base = g * pitch + PAD
        row = jnp.concatenate([taps_ref[g : g + 1, :], jnp.zeros((1, TILE), jnp.float32)], 1)
        sheared = pltpu.roll(jnp.broadcast_to(row, (TILE, span + TILE)), 0, 1, stride=1, stride_axis=0)
        for t in range(tiles):
            toep[g, t * TILE : (t + 1) * TILE, :] = sheared[:, t * TILE : (t + 1) * TILE].astype(jnp.bfloat16)
        lefts = [
            [
                (
                    spread[h, base : base + rows_b, :]
                    if lag == 0
                    else jnp.where(behind >= lag, spread[h, base - lag : base - lag + rows_b, :], 0.0)
                ).astype(jnp.bfloat16)
                for h in range(2)
            ]
            for lag in range(lags)
        ]
        last = lags - 1
        both = jnp.concatenate([lefts[last][0], lefts[0][1]], 0)
        both = jnp.dot(both, jnp.concatenate([tile(g, 2 * last), tile(g, 0)], 1), preferred_element_type=jnp.float32)
        total = jnp.concatenate([both[:rows_b, :TILE], both[rows_b:, TILE:]], 1)
        for lag in range(last):
            t = 2 * lag
            if lag == 0:
                left = [lefts[0][0], lefts[last][1]]
                lower = [tile(g, 2 * last - 1), tile(g, 2 * last)]
            else:
                left = lefts[lag]
                lower = [tile(g, t - 1), tile(g, t)]
            right = [jnp.concatenate([tile(g, t), tile(g, t + 1)], 1), jnp.concatenate(lower, 1)]
            total = total + jnp.dot(
                jnp.concatenate(left, 1), jnp.concatenate(right, 0), preferred_element_type=jnp.float32
            )
        for h in range(2):
            result[h, g * held : g * held + rows, :] = total[:rows, h * TILE : (h + 1) * TILE]

    def slab_of(row):
        return jnp.concatenate([result[h, pl.ds(row, channels, stride=held), :] for h in range(2)], 1)

    for block in range(devices):
        out_ref[block] = slab_of(heads[0, block]).astype(jnp.bfloat16)
    for prompt in range(lengths_ref.shape[0]):
        row = heads[1, prompt]
        block = table[0, row]
        old = out_ref[block].astype(jnp.float32)
        out_ref[block] = only_lanes(table, row, slab_of(row), old).astype(jnp.bfloat16)


def round_up(value, to):
    return -(-value // to) * to


def long_conv(lengths, signal, taps, short_taps):
    devices, tok_rows = signal.shape[0], BLK
    channels = taps.shape[0]
    shape = (devices, channels, tok_rows)
    span = taps.shape[1]
    rows = round_up(devices + lengths.shape[0] - 1, 8)
    rows_b = round_up(rows, 16)
    return pl.pallas_call(
        functools.partial(conv_kernel, rows=rows, rows_b=rows_b),
        grid=(1,),
        out_shape=jax.ShapeDtypeStruct(shape, jnp.bfloat16),
        in_specs=[
            pl.BlockSpec(memory_space=pltpu.SMEM),
            pl.BlockSpec(signal.shape, lambda i: (0, 0, 0)),
            pl.BlockSpec((channels, span), lambda i: (0, 0)),
            pl.BlockSpec(short_taps.shape, lambda i: (0, 0, 0)),
        ],
        out_specs=pl.BlockSpec(shape, lambda i: (0, 0, 0)),
        scratch_shapes=[
            pltpu.SMEM((3, rows), jnp.int32),
            pltpu.SMEM((2, devices), jnp.int32),
            pltpu.VMEM(shape, jnp.float32),
            pltpu.VMEM((devices * EDGES, TILE), jnp.float32),
            pltpu.VMEM((2, round_up(channels * pitch_of(PAD + rows_b), 8), TILE), jnp.float32),
            pltpu.VMEM((2, round_up(channels * pitch_of(rows), 8), TILE), jnp.float32),
            pltpu.VMEM((rows_b, TILE), jnp.int32),
            pltpu.VMEM((channels, span + TILE, TILE), jnp.bfloat16),
        ],
        compiler_params=params(GRANT),
        cost_estimate=pl.CostEstimate(
            flops=2 * channels * rows * (span + BLK) * BLK, bytes_accessed=2 * MIB, transcendentals=0
        ),
    )(lengths, signal, taps, short_taps)


def gate_kernel(query_ref, conv_ref, *out_refs):
    conv = conv_ref[...].astype(jnp.float32).T
    gated = (query_ref[...].astype(jnp.float32) * conv).astype(jnp.bfloat16)
    rows = gated.shape[0] // len(out_refs)
    for i, out_ref in enumerate(out_refs):
        out_ref[...] = gated[i * rows : (i + 1) * rows]


def gate(query, conv_t, pieces=2, width=1024):
    tok_rows, channels = query.shape
    width = min(width, channels)
    rows = tok_rows // pieces
    return pl.pallas_call(
        gate_kernel,
        grid=(channels // width,),
        out_shape=[jax.ShapeDtypeStruct((rows, channels), jnp.bfloat16)] * pieces,
        in_specs=[
            pl.BlockSpec((tok_rows, width), lambda i: (0, i)),
            pl.BlockSpec((width, tok_rows), lambda i: (i, 0)),
        ],
        out_specs=[pl.BlockSpec((rows, width), lambda i: (0, i))] * pieces,
        compiler_params=params(GRANT),
        cost_estimate=pl.CostEstimate(flops=tok_rows * channels, bytes_accessed=2 * MIB, transcendentals=0),
    )(query, conv_t)


def shift(array, axis, by):
    length = lax.axis_size(axis)
    return lax.ppermute(array, axis, [(i, (i + by) % length) for i in range(length)])


def project_kernel(*refs, count, pieces, has_total):
    blocks, weights = refs[: count * pieces], refs[count * pieces : count * (pieces + 1)]
    out_ref = refs[-1]
    total = refs[count * (pieces + 1)][...] if has_total else None
    for i in range(count):
        block = jnp.concatenate([ref[...] for ref in blocks[i * pieces : (i + 1) * pieces]], 0)
        term = jnp.dot(block, weights[i][...], preferred_element_type=jnp.float32)
        total = term if total is None else total + term
    out_ref[...] = total.astype(out_ref.dtype)


def project_part(blocks, weights, total, kind):
    count, pieces = len(blocks), len(blocks[0])
    rows, depth = blocks[0][0].shape
    columns = weights[0].shape[1]
    tok_rows = rows * pieces
    operands = [piece for block in blocks for piece in block] + weights + ([] if total is None else [total])
    return pl.pallas_call(
        functools.partial(project_kernel, count=count, pieces=pieces, has_total=total is not None),
        out_shape=jax.ShapeDtypeStruct((tok_rows, columns), kind),
        compiler_params=params(GRANT),
        cost_estimate=pl.CostEstimate(
            flops=2 * count * tok_rows * depth * columns,
            bytes_accessed=2 * count * depth * columns,
            transcendentals=0,
        ),
    )(*operands)


def project(pieces, w_out):
    size = lax.axis_size("ch")
    place = lax.axis_index("ch")
    depth = pieces[0].shape[1]
    own, after, far_rows, before = (
        lax.dynamic_slice_in_dim(w_out, (place + i) % size * depth, depth, 0) for i in range(size)
    )
    up, down = pieces
    right_up, left_down = shift(up, "ch", 1), shift(down, "ch", -1)
    right_down, left_up = shift(down, "ch", 1), shift(up, "ch", -1)
    far_up, far_down = shift(right_up, "ch", 1), shift(left_down, "ch", -1)
    total = project_part([(up, down)], [own], None, jnp.float32)
    near = [(right_up, right_down), (left_up, left_down)]
    total = project_part(near, [before, after], total, jnp.float32)
    return project_part([(far_up, far_down)], [far_rows], total, jnp.bfloat16)


def per_device(qkv, short_taps, lengths, filter_taps, w_out):
    tok_rows, _, width = qkv.shape
    lead = TAPS - 1
    seq = lax.axis_size("seq")
    by_kind = qkv.transpose(1, 0, 2)
    sent = products(lengths, by_kind, short_taps, seq)
    signal = lax.all_to_all(sent, "seq", 0, 0, tiled=True)
    conv = long_conv(lengths, signal, filter_taps[0], short_taps)
    late, conv = lax.optimization_barrier((by_kind, conv))
    edge = lax.ppermute(late[0, tok_rows - lead :], "seq", [(i, i + 1) for i in range(seq - 1)])
    query = queries(lengths, late, edge, short_taps)
    conv_t = lax.all_to_all(conv, "seq", 0, 0, tiled=True).reshape(width, tok_rows)
    return project(gate(query, conv_t), w_out)


def solution(mesh):
    placed = (P("seq", None, "ch"), P(None, None, "ch"), P(), P("ch", "seq", None), P(None, "ch"))
    return jax.shard_map(
        per_device, mesh=mesh, in_specs=placed, out_specs=P("seq", "ch"), check_vma=False
    )
```
